128 devices in a mesh: bucket: 32 (over z, y, core), dom: 4 (over x).
Axes of the slice: x: 4, y: 4, z: 4, core: 2. Of those that a mesh axis runs over, the one named last changes fastest.
Arguments:
- left_table: float32 [262144, 128], P(('bucket', 'dom')), may hold values from -1.8 to 1.8
- right_table: float32 [262144, 128], P(('bucket', 'dom')), may hold values from -1.8 to 1.8
- left_state: float32 [262144], P(('bucket', 'dom')), may hold values from 0.01 to 1
- right_state: float32 [262144], P(('bucket', 'dom')), may hold values from 0.01 to 1
- sources: int32 [2097152], P(('bucket', 'dom')), may hold values from 0 to 8191
- targets: int32 [2097152], P(('bucket', 'dom')), may hold values from 0 to 8191
- relation_ids: int32 [2097152], P(('bucket', 'dom')), may hold values from 0 to 8191
- negatives: int32 [4096, 1024], P(('bucket', 'dom')), may hold values from 0 to 8191
- rotation: int32 [1], replicated, may hold values from 0 to 31
- relations: float32 [8192, 128], replicated, may hold values from -4 to 4
- relation_state: float32 [8192], replicated, may hold values from 0.01 to 1
Outputs:
- left_updated: float32 [262144, 128], P(('bucket', 'dom'))
- right_updated: float32 [262144, 128], P(('bucket', 'dom'))
- left_accum: float32 [262144], P(('bucket', 'dom'))
- right_accum: float32 [262144], P(('bucket', 'dom'))
- relations_updated: float32 [8192, 128], replicated
- relation_accum: float32 [8192], replicated
The draws below stay inside these ranges and needn't reach their ends.
Inputs may be any that keep to these rules, and one draw needn't show every extreme that they name: Trainer b pairs left partition b with right partition (b + rotation) mod 32.
All inputs are finite; a program needn't handle non-finite values.
Results may differ from the reference program's by a relative error of at most 0.00012.
Values sent between devices are 32-bit elements; how exact they have to be, the bound alone decides.
A program may use at most 128 MiB of HBM per device.

```python
import math
import jax
import jax.numpy as jnp
import numpy as np
from jax import lax

DIM = 128
REL = 8192
NEG = 1024
SPAN = 512
SPANS = 32
PART = 8192
HALF = 262144
EDGES = 2097152
BLOCKS = 4096
N_BUCKET = 32
N_DOM = 4


def place_ends(drawn, rng, least, high):
    spot = [jax.random.randint(jax.random.fold_in(rng, axis), (), 0, length) for axis, length in enumerate(drawn.shape)]
    main_axis = drawn.shape.index(max(drawn.shape))
    next_to = spot[:main_axis] + [(spot[main_axis] + 1) % drawn.shape[main_axis]] + spot[main_axis + 1:]
    return drawn.at[tuple(spot)].set(least).at[tuple(next_to)].set(high)


def shard_levels(stream_key, extent, shards, low, largest):
    gain, own = 1.0, jax.random.fold_in(stream_key, 6)
    for axis_at, shards_of in shards:
        draws = jnp.exp(jax.random.uniform(jax.random.fold_in(own, axis_at), (shards_of,), jnp.float32, low / len(shards), largest / len(shards)))
        gain = gain * jnp.repeat(draws, extent[axis_at] // shards_of).reshape([-1 if axis == axis_at else 1 for axis in range(len(extent))])
    return gain


def rank_table(amount, skew):
    portions = [(1 << 20) // math.isqrt(grade ** skew) + 1 for grade in range(1, amount + 1)]
    scale = 1 + sum(portions) // (1 << 30)
    return np.cumsum(np.array([max(1, weight // scale) for weight in portions]))


def skewed_ids(own_key, extent, count, skew):
    table = rank_table(count, skew)
    ticket = jax.random.randint(jax.random.fold_in(own_key, 1), extent, 0, int(table[count - 1]))
    grade = jnp.searchsorted(jnp.asarray(table, jnp.int32), ticket, side="right")
    return jax.random.permutation(jax.random.fold_in(own_key, 2), count)[grade].astype(jnp.int32)


def gaussian(stream_key, shape, width, bound, shards=(), dtype=jnp.bfloat16):
    entries = width * jax.random.normal(stream_key, shape, jnp.float32)
    if shards:
        entries = entries * shard_levels(stream_key, shape, shards, -0.22, 0.18)
    return jnp.clip(entries, -bound, bound).astype(dtype)


def setup_inputs(seed: int = 0) -> dict:
    splits = jax.random.split(jax.random.key(seed), 12)
    return {
        "left_table": gaussian(splits[0], (HALF, DIM), 0.3, 1.8, ((0, 128),), jnp.float32),
        "right_table": gaussian(splits[1], (HALF, DIM), 0.3, 1.8, ((0, 128),), jnp.float32),
        "left_state": jnp.clip(jnp.exp(math.log(1.0) - 4.6051702 * jax.random.uniform(splits[2], (HALF,), jnp.float32) ** shard_levels(splits[2], (HALF,), ((0, 128),), -0.2, 0.2)), 0.01, 1.0),
        "right_state": jnp.clip(jnp.exp(math.log(1.0) - 4.6051702 * jax.random.uniform(splits[3], (HALF,), jnp.float32) ** shard_levels(splits[3], (HALF,), ((0, 128),), -0.2, 0.2)), 0.01, 1.0),
        "sources": place_ends(jax.random.randint(splits[4], (EDGES,), 0, PART), jax.random.fold_in(splits[4], 1), 0, PART - 1).astype(jnp.int32),
        "targets": place_ends(skewed_ids(splits[5], (EDGES,), PART, 2), jax.random.fold_in(splits[5], 3), 0, PART - 1).astype(jnp.int32),
        "relation_ids": place_ends(skewed_ids(splits[6], (EDGES,), REL, 2), jax.random.fold_in(splits[6], 3), 0, REL - 1).astype(jnp.int32),
        "negatives": place_ends(jax.random.randint(splits[7], (BLOCKS, NEG), 0, PART), jax.random.fold_in(splits[7], 1), 0, PART - 1).astype(jnp.int32),
        "rotation": jax.random.randint(splits[8], (1,), 0, N_BUCKET).astype(jnp.int32),
        "relations": gaussian(splits[9], (REL, DIM), 1.0, 4.0, (), jnp.float32),
        "relation_state": jnp.clip(jnp.exp(jax.random.uniform(splits[10], (REL,), jnp.float32, math.log(0.01), math.log(1.0))), 0.01, 1.0),
    }


learn_rate = 0.2
margin_gap = 1.0

def adagrad(param, state, grad):
    new_state = state + lax.optimization_barrier(jnp.mean(grad * grad, axis=-1))
    return (param - learn_rate * grad / jnp.sqrt(new_state)[:, None], new_state)

def span_terms(left_part, right_part, relations, src_rows, dst_rows, rel_rows, neg_rows):
    high = lax.Precision.HIGHEST
    left_vec = left_part[src_rows]
    right_vec = right_part[dst_rows]
    operator = relations[rel_rows]
    query = left_vec * operator
    negative = right_part[neg_rows]
    positive = lax.optimization_barrier(jnp.sum(query * right_vec, axis=-1))
    scores = jnp.dot(query, negative.T, precision=high)
    weights = jax.nn.sigmoid(scores - positive[:, None] + margin_gap) / NEG
    total = lax.optimization_barrier(jnp.sum(weights, axis=-1))
    grad_query = jnp.dot(weights, negative, precision=high) - total[:, None] * right_vec
    grad_neg = jnp.dot(weights.T, query, precision=high)
    grad_right = -total[:, None] * query
    return (grad_query * operator, grad_right, grad_neg, grad_query * left_vec)

def reference(left_table, right_table, left_state, right_state, sources, targets, relation_ids, negatives, rotation, relations, relation_state):
    shift = rotation[0]
    left_parts = left_table.reshape(N_BUCKET, PART, DIM)
    right_parts = jnp.roll(right_table.reshape(N_BUCKET, PART, DIM), -shift, axis=0)
    left_sums = left_state.reshape(N_BUCKET, PART)
    right_sums = jnp.roll(right_state.reshape(N_BUCKET, PART), -shift, axis=0)
    src_all = sources.reshape(N_BUCKET, N_DOM * SPANS, SPAN)
    dst_all = targets.reshape(N_BUCKET, N_DOM * SPANS, SPAN)
    rel_all = relation_ids.reshape(N_BUCKET, N_DOM * SPANS, SPAN)
    neg_all = negatives.reshape(N_BUCKET, N_DOM * SPANS, NEG)

    def trainer(items):
        left_part, right_part, left_acc, right_acc, src_b, dst_b, rel_b, neg_b = items

        def step(carry, span):
            return (carry, span_terms(left_part, right_part, relations, span[0], span[1], span[2], span[3]))
        unused, grads = lax.scan(step, 0, (src_b, dst_b, rel_b, neg_b))
        grad_left, grad_right, grad_neg, grad_rel = grads
        left_grad = jax.ops.segment_sum(grad_left.reshape(-1, DIM), src_b.reshape(-1), PART)
        right_grad = jax.ops.segment_sum(grad_right.reshape(-1, DIM), dst_b.reshape(-1), PART)
        right_grad = right_grad + jax.ops.segment_sum(grad_neg.reshape(-1, DIM), neg_b.reshape(-1), PART)
        rel_grad = jax.ops.segment_sum(grad_rel.reshape(-1, DIM), rel_b.reshape(-1), REL)
        new_left, new_left_acc = adagrad(left_part, left_acc, left_grad)
        new_right, new_right_acc = adagrad(right_part, right_acc, right_grad)
        return (new_left, new_left_acc, new_right, new_right_acc, rel_grad)
    outputs = lax.map(trainer, (left_parts, right_parts, left_sums, right_sums, src_all, dst_all, rel_all, neg_all))
    new_left, new_left_acc, new_right, new_right_acc, rel_grads = outputs
    rel_total = lax.optimization_barrier(jnp.sum(rel_grads, axis=0))
    new_right = jnp.roll(new_right, shift, axis=0).reshape(HALF, DIM)
    new_right_acc = jnp.roll(new_right_acc, shift, axis=0).reshape(HALF)
    new_rel, new_rel_acc = adagrad(relations, relation_state, rel_total)
    return (new_left.reshape(HALF, DIM), new_right, new_left_acc.reshape(HALF), new_right_acc, new_rel, new_rel_acc)
```

```python
import jax
import jax.numpy as jnp
from jax import lax
from jax.experimental import pallas as pl
from jax.experimental.pallas import tpu as pltpu
from jax.sharding import PartitionSpec as P

learn_rate = 0.2
margin_gap = 1.0
TILE = 256
NT = (((1,), (1,)), ((), ()))
NN = (((1,), (0,)), ((), ()))


def adagrad(param, state, grad):
    new_state = state + jnp.mean(grad * grad, axis=-1)
    return (param - learn_rate * grad / jnp.sqrt(new_state)[:, None], new_state)


def rotate(array, amount):
    size = lax.axis_size("bucket")

    def move(by):
        if by == 0:
            return lambda a: a
        return lambda a: lax.ppermute(a, "bucket", [(i, (i - by) % size) for i in range(size)])

    return lax.switch(amount, [move(by) for by in range(size)], array)


def split(a):
    hi = a.astype(jnp.bfloat16)
    return hi, (a - hi.astype(jnp.float32)).astype(jnp.bfloat16)


def dot(a, b, dims=NN):
    return lax.dot_general(a, b, dims, preferred_element_type=jnp.float32)


def local_grads(src, dst, rid, neg, left, right, rel, span_len):
    span_count, neg_count = neg.shape
    neg = neg.reshape(-1)
    width = left.shape[1]
    tile = min(TILE, span_len)
    per = neg_count // span_len

    def kernel(src, dst, rid, neg, left, right, rel, gl, gr, grel, x, r, y, n, gx, gy, gg, gn):
        gl[...] = jnp.zeros_like(gl)
        gr[...] = jnp.zeros_like(gr)
        grel[...] = jnp.zeros_like(grel)

        @pl.loop(0, span_count)
        def _(b):
            @pl.loop(0, span_len // 8)
            def _(i):
                e0 = pl.multiple_of(i * 8, 8)
                n0 = pl.multiple_of(i * 8 * per, 8 * per)
                for s in range(8):
                    e = b * span_len + e0 + s
                    x[pl.ds(e0 + s, 1), :] = left[pl.ds(src[e], 1), :]
                    r[pl.ds(e0 + s, 1), :] = rel[pl.ds(rid[e], 1), :]
                    y[pl.ds(e0 + s, 1), :] = right[pl.ds(dst[e], 1), :]
                    for k in range(per):
                        m = n0 + per * s + k
                        n[pl.ds(m, 1), :] = right[pl.ds(neg[b * neg_count + m], 1), :]

            nh, nl = split(n[...])
            ncat = jnp.concatenate([nh, nl], axis=1)
            acc = jnp.zeros((2 * width, neg_count), jnp.float32)
            acc2 = jnp.zeros((width, neg_count), jnp.float32)
            for t in range(span_len // tile):
                rows = pl.ds(t * tile, tile)
                xv, rv, yv = x[rows, :], r[rows, :], y[rows, :]
                q = xv * rv
                pos = jnp.sum(q * yv, axis=1, keepdims=True)
                qh, ql = split(q)
                score = dot(jnp.concatenate([qh, ql], axis=1), jnp.concatenate([nh, nh], axis=1), NT) + dot(qh, nl, NT)
                w = jax.nn.sigmoid(score + (margin_gap - pos))
                total = jnp.sum(w, axis=1, keepdims=True) * (1.0 / neg_count)
                wh, wl = split(w)
                a = dot(wh, ncat)
                gq = (a[:, :width] + a[:, width:] + dot(wl, nh)) * (1.0 / neg_count) - total * yv
                gx[rows, :] = gq * rv
                gg[rows, :] = gq * xv
                gy[rows, :] = -total * q
                qth, qtl = split(q.T)
                acc += dot(jnp.concatenate([qth, qtl], axis=0), wh)
                acc2 += dot(qth, wl)
            gn[...] = ((acc[:width] + acc[width:] + acc2) * (1.0 / neg_count)).T

            @pl.loop(0, span_len // 8)
            def _(i):
                e0 = pl.multiple_of(i * 8, 8)
                n0 = pl.multiple_of(i * 8 * per, 8 * per)
                for s in range(8):
                    e = b * span_len + e0 + s
                    gl[pl.ds(src[e], 1), :] += gx[pl.ds(e0 + s, 1), :]
                    grel[pl.ds(rid[e], 1), :] += gg[pl.ds(e0 + s, 1), :]
                    gr[pl.ds(dst[e], 1), :] += gy[pl.ds(e0 + s, 1), :]
                    for k in range(per):
                        m = n0 + per * s + k
                        gr[pl.ds(neg[b * neg_count + m], 1), :] += gn[pl.ds(m, 1), :]

    scalars = pl.BlockSpec(memory_space=pltpu.SMEM)
    whole = pl.BlockSpec(memory_space=pltpu.VMEM)
    edge = pltpu.VMEM((span_len, width), jnp.float32)
    negs = pltpu.VMEM((neg_count, width), jnp.float32)
    return pl.pallas_call(
        kernel,
        out_shape=[jax.ShapeDtypeStruct(a.shape, jnp.float32) for a in (left, right, rel)],
        in_specs=[scalars] * 4 + [whole] * 3,
        out_specs=[whole] * 3,
        scratch_shapes=[edge, edge, edge, negs, edge, edge, edge, negs],
        compiler_params=pltpu.CompilerParams(vmem_limit_bytes=60 * 1024 * 1024),
        name="local_grads",
    )(src, dst, rid, neg, left, right, rel)


def body(
    left_table,
    right_table,
    left_state,
    right_state,
    sources,
    targets,
    relation_ids,
    negatives,
    rotation,
    relations,
    relation_state,
):
    trainers = lax.axis_size("bucket")
    left_full = lax.all_gather(left_table, "dom", axis=0, tiled=True)
    right_rows = rotate(right_table, jnp.mod(rotation[0], trainers))
    right_full = lax.all_gather(right_rows, "dom", axis=0, tiled=True)
    span_len = sources.shape[0] // negatives.shape[0]
    left_grad, right_grad, rel_grad = local_grads(
        sources, targets, relation_ids, negatives, left_full, right_full, relations, span_len
    )
    everyone = ("bucket", "dom")
    right_share = lax.psum_scatter(right_grad, "dom", scatter_dimension=0, tiled=True)
    left_share = lax.psum_scatter(left_grad, "dom", scatter_dimension=0, tiled=True)
    right_share = rotate(right_share, jnp.mod(-rotation[0], trainers))
    new_left, new_left_acc = adagrad(left_table, left_state, left_share)
    new_right, new_right_acc = adagrad(right_table, right_state, right_share)
    rel_share = lax.psum_scatter(rel_grad, everyone, scatter_dimension=0, tiled=True)
    rel_total = lax.all_gather(rel_share, everyone, axis=0, tiled=True)
    new_rel, new_rel_acc = adagrad(relations, relation_state, rel_total)
    return (new_left, new_right, new_left_acc, new_right_acc, new_rel, new_rel_acc)


def solution(mesh):
    both = ("bucket", "dom")
    return jax.shard_map(
        body,
        mesh=mesh,
        in_specs=(
            P(both, None),
            P(both, None),
            P(both),
            P(both),
            P(both),
            P(both),
            P(both),
            P(both, None),
            P(),
            P(),
            P(),
        ),
        out_specs=(P(both, None), P(both, None), P(both), P(both), P(), P()),
        check_vma=False,
    )
```

```python
import math

import jax
import jax.numpy as jnp
from jax import lax
from jax.experimental import pallas as pl
from jax.experimental.pallas import tpu as pltpu
from jax.sharding import PartitionSpec as P

learn_rate = 0.2
margin_gap = 1.0
TILE = 256
MESH = pl.DeviceIdType.MESH
CORES, SIDE = 2, 4
SIZES = {"core": CORES, "y": SIDE, "z": SIDE, "x": SIDE}
ORDERS = (("core", "y", "z", "x"), ("core", "z", "y", "x"))
NT = (((1,), (1,)), ((), ()))
NN = (((1,), (0,)), ((), ()))


def adagrad(param, state, grad):
    new_state = state + jnp.mean(grad * grad, axis=-1)
    return (param - learn_rate * grad / jnp.sqrt(new_state)[:, None], new_state)


def rotate(array, amount):
    size = lax.axis_size("bucket")

    def move(by):
        if by == 0:
            return lambda a: a
        return lambda a: lax.ppermute(a, "bucket", [(i, (i - by) % size) for i in range(size)])

    return lax.switch(amount, [move(by) for by in range(size)], array)


def split(a):
    hi = a.astype(jnp.bfloat16)
    return hi, (a - hi.astype(jnp.float32)).astype(jnp.bfloat16)


def dot(a, b, dims=NN):
    return lax.dot_general(a, b, dims, preferred_element_type=jnp.float32)


def local_grads(src, dst, rid, neg, left, right, rel, span_len):
    span_count, neg_count = neg.shape
    neg = neg.reshape(-1)
    width = left.shape[1]
    tile = min(TILE, span_len)
    per = neg_count // span_len

    def kernel(src, dst, rid, neg, left, right, rel, gl, gr, grel, x, r, y, n, gx, gy, gg, gn):
        gl[...] = jnp.zeros_like(gl)
        gr[...] = jnp.zeros_like(gr)
        grel[...] = jnp.zeros_like(grel)

        @pl.loop(0, span_count)
        def _(b):
            @pl.loop(0, span_len // 8)
            def _(i):
                e0 = pl.multiple_of(i * 8, 8)
                n0 = pl.multiple_of(i * 8 * per, 8 * per)
                for s in range(8):
                    e = b * span_len + e0 + s
                    x[pl.ds(e0 + s, 1), :] = left[pl.ds(src[e], 1), :]
                    r[pl.ds(e0 + s, 1), :] = rel[pl.ds(rid[e], 1), :]
                    y[pl.ds(e0 + s, 1), :] = right[pl.ds(dst[e], 1), :]
                    for k in range(per):
                        m = n0 + per * s + k
                        n[pl.ds(m, 1), :] = right[pl.ds(neg[b * neg_count + m], 1), :]

            nh, nl = split(n[...])
            ncat = jnp.concatenate([nh, nl], axis=1)
            acc = jnp.zeros((2 * width, neg_count), jnp.float32)
            acc2 = jnp.zeros((width, neg_count), jnp.float32)
            for t in range(span_len // tile):
                rows = pl.ds(t * tile, tile)
                xv, rv, yv = x[rows, :], r[rows, :], y[rows, :]
                q = xv * rv
                pos = jnp.sum(q * yv, axis=1, keepdims=True)
                qh, ql = split(q)
                score = dot(jnp.concatenate([qh, ql], axis=1), jnp.concatenate([nh, nh], axis=1), NT) + dot(qh, nl, NT)
                w = jax.nn.sigmoid(score + (margin_gap - pos))
                total = jnp.sum(w, axis=1, keepdims=True) * (1.0 / neg_count)
                wh, wl = split(w)
                a = dot(wh, ncat)
                gq = (a[:, :width] + a[:, width:] + dot(wl, nh)) * (1.0 / neg_count) - total * yv
                gx[rows, :] = gq * rv
                gg[rows, :] = gq * xv
                gy[rows, :] = -total * q
                qth, qtl = split(q.T)
                acc += dot(jnp.concatenate([qth, qtl], axis=0), wh)
                acc2 += dot(qth, wl)
            gn[...] = ((acc[:width] + acc[width:] + acc2) * (1.0 / neg_count)).T

            @pl.loop(0, span_len // 8)
            def _(i):
                e0 = pl.multiple_of(i * 8, 8)
                n0 = pl.multiple_of(i * 8 * per, 8 * per)
                for s in range(8):
                    e = b * span_len + e0 + s
                    gl[pl.ds(src[e], 1), :] += gx[pl.ds(e0 + s, 1), :]
                    grel[pl.ds(rid[e], 1), :] += gg[pl.ds(e0 + s, 1), :]
                    gr[pl.ds(dst[e], 1), :] += gy[pl.ds(e0 + s, 1), :]
                    for k in range(per):
                        m = n0 + per * s + k
                        gr[pl.ds(neg[b * neg_count + m], 1), :] += gn[pl.ds(m, 1), :]

    scalars = pl.BlockSpec(memory_space=pltpu.SMEM)
    whole = pl.BlockSpec(memory_space=pltpu.VMEM)
    edge = pltpu.VMEM((span_len, width), jnp.float32)
    negs = pltpu.VMEM((neg_count, width), jnp.float32)
    return pl.pallas_call(
        kernel,
        out_shape=[jax.ShapeDtypeStruct(a.shape, jnp.float32) for a in (left, right, rel)],
        in_specs=[scalars] * 4 + [whole] * 3,
        out_specs=[whole] * 3,
        scratch_shapes=[edge, edge, edge, negs, edge, edge, edge, negs],
        compiler_params=pltpu.CompilerParams(vmem_limit_bytes=60 * 1024 * 1024),
        name="local_grads",
    )(src, dst, rid, neg, left, right, rel)


def split_place(bucket):
    core = lax.rem(bucket, CORES)
    chip = lax.div(bucket, CORES)
    return {"core": core, "y": lax.rem(chip, SIDE), "z": lax.div(chip, SIDE), "x": lax.axis_index("dom")}


def peer_of(place, axis, by):
    size = SIZES[axis]
    spot = dict(place)
    spot[axis] = lax.rem(place[axis] + by, size)
    return {"bucket": (spot["z"] * SIDE + spot["y"]) * CORES + spot["core"], "dom": spot["x"]}


def sum_everywhere(grads):
    rows, width = grads.shape
    half = rows // len(ORDERS)

    def kernel(grad, out, *scratch):
        levels = len(ORDERS[0])
        parts = [scratch[k * levels : (k + 1) * levels] for k in range(len(ORDERS))]
        arrived = [scratch[(len(ORDERS) + k) * levels : (len(ORDERS) + k + 1) * levels] for k in range(len(ORDERS))]
        send_in, recv_in, send_out, recv_out = scratch[2 * len(ORDERS) * levels :]
        place = split_place(lax.axis_index("bucket"))
        barrier = pltpu.get_barrier_semaphore()
        greeted = 0
        for axis, size in SIZES.items():
            for by in range(1, size):
                pl.semaphore_signal(barrier, inc=1, device_id=peer_of(place, axis, by), device_id_type=MESH)
                greeted += 1
        pl.semaphore_wait(barrier, greeted)

        def copy(source, target, sends, recvs, k, level, by, axis):
            return pltpu.make_async_remote_copy(
                src_ref=source,
                dst_ref=target,
                send_sem=sends.at[k, level, by],
                recv_sem=recvs.at[k, level, by],
                device_id=peer_of(place, axis, by),
                device_id_type=MESH,
            )

        lows = [k * half for k in range(len(ORDERS))]
        starts = [[] for _ in ORDERS]
        for level in range(levels):
            copies = []
            for k, order in enumerate(ORDERS):
                axis = order[level]
                size = SIZES[axis]
                block = half // math.prod(SIZES[a] for a in order[: level + 1])
                source = grad if level == 0 else parts[k][level - 1]
                base = lows[k] if level == 0 else 0
                for by in range(1, size):
                    other = lax.rem(place[axis] + by, size)
                    c = copy(
                        source.at[pl.ds(pl.multiple_of(base + other * block, 8), block), :],
                        arrived[k][level].at[by - 1],
                        send_in, recv_in, k, level, by, axis,
                    )
                    c.start()
                    copies.append(c)
            for c in copies:
                c.wait()
            for k, order in enumerate(ORDERS):
                axis = order[level]
                size = SIZES[axis]
                block = half // math.prod(SIZES[a] for a in order[: level + 1])
                source = grad if level == 0 else parts[k][level - 1]
                base = lows[k] if level == 0 else 0
                own = source[pl.ds(pl.multiple_of(base + place[axis] * block, 8), block), :]
                for by in range(1, size):
                    own = own + arrived[k][level][by - 1]
                starts[k].append(place[axis] * block)
                if level < levels - 1:
                    parts[k][level][...] = own
                else:
                    first = lows[k] + sum(starts[k])
                    out[pl.ds(pl.multiple_of(first, 8), block), :] = own
        for level in reversed(range(levels)):
            copies = []
            for k, order in enumerate(ORDERS):
                axis = order[level]
                block = half // math.prod(SIZES[a] for a in order[: level + 1])
                first = lows[k] + sum(starts[k][: level + 1])
                where = out.at[pl.ds(pl.multiple_of(first, 8), block), :]
                for by in range(1, SIZES[axis]):
                    c = copy(where, where, send_out, recv_out, k, level, by, axis)
                    c.start()
                    copies.append(c)
            for c in copies:
                c.wait()

    parts, arrived = [], []
    for order in ORDERS:
        for level in range(len(order)):
            block = half // math.prod(SIZES[a] for a in order[: level + 1])
            parts.append(pltpu.VMEM((block, width), jnp.float32))
            arrived.append(pltpu.VMEM((SIZES[order[level]] - 1, block, width), jnp.float32))
    whole = pl.BlockSpec(memory_space=pltpu.VMEM)
    sems = pltpu.SemaphoreType.DMA((len(ORDERS), len(ORDERS[0]), SIDE))
    return pl.pallas_call(
        kernel,
        out_shape=jax.ShapeDtypeStruct(grads.shape, jnp.float32),
        in_specs=[whole],
        out_specs=whole,
        scratch_shapes=parts + arrived + [sems] * 4,
        compiler_params=pltpu.CompilerParams(
            collective_id=0, has_side_effects=True, vmem_limit_bytes=40 * 1024 * 1024
        ),
        cost_estimate=pl.CostEstimate(flops=2 * rows * width, bytes_accessed=40 * rows * width, transcendentals=0),
        name="relation_sums",
    )(grads)


def body(
    left_table,
    right_table,
    left_state,
    right_state,
    sources,
    targets,
    relation_ids,
    negatives,
    rotation,
    relations,
    relation_state,
):
    trainers = lax.axis_size("bucket")
    left_full = lax.all_gather(left_table, "dom", axis=0, tiled=True)
    right_rows = rotate(right_table, jnp.mod(rotation[0], trainers))
    right_full = lax.all_gather(right_rows, "dom", axis=0, tiled=True)
    span_len = sources.shape[0] // negatives.shape[0]
    left_grad, right_grad, rel_grad = local_grads(
        sources, targets, relation_ids, negatives, left_full, right_full, relations, span_len
    )
    right_share = lax.psum_scatter(right_grad, "dom", scatter_dimension=0, tiled=True)
    left_share = lax.psum_scatter(left_grad, "dom", scatter_dimension=0, tiled=True)
    right_share = rotate(right_share, jnp.mod(-rotation[0], trainers))
    new_left, new_left_acc = adagrad(left_table, left_state, left_share)
    new_right, new_right_acc = adagrad(right_table, right_state, right_share)
    rel_total = sum_everywhere(rel_grad)
    new_rel, new_rel_acc = adagrad(relations, relation_state, rel_total)
    return (new_left, new_right, new_left_acc, new_right_acc, new_rel, new_rel_acc)


def solution(mesh):
    both = ("bucket", "dom")
    return jax.shard_map(
        body,
        mesh=mesh,
        in_specs=(
            P(both, None),
            P(both, None),
            P(both),
            P(both),
            P(both),
            P(both),
            P(both),
            P(both, None),
            P(),
            P(),
            P(),
        ),
        out_specs=(P(both, None), P(both, None), P(both), P(both), P(), P()),
        check_vma=False,
    )
```

```python
import math

import jax
import jax.numpy as jnp
from jax import lax
from jax.experimental import pallas as pl
from jax.experimental.pallas import tpu as pltpu
from jax.sharding import PartitionSpec as P

learn_rate = 0.2
margin_gap = 1.0
TILE = 256
VMEM_LIMIT = 60 * 1024 * 1024
MESH = pl.DeviceIdType.MESH
CORES, SIDE = 2, 4
SIZES = {"core": CORES, "y": SIDE, "z": SIDE, "x": SIDE}
ORDERS = (("core", "y", "z", "x"), ("core", "z", "y", "x"))
NT = (((1,), (1,)), ((), ()))
NN = (((1,), (0,)), ((), ()))


def adagrad(param, state, grad):
    new_state = state + jnp.mean(grad * grad, axis=-1)
    return (param - learn_rate * grad / jnp.sqrt(new_state)[:, None], new_state)


def rotate(array, amount):
    size = lax.axis_size("bucket")

    def move(by):
        if by == 0:
            return lambda a: a
        return lambda a: lax.ppermute(a, "bucket", [(i, (i - by) % size) for i in range(size)])

    return lax.switch(amount, [move(by) for by in range(size)], array)


def split(a):
    hi = a.astype(jnp.bfloat16)
    return hi, (a - hi.astype(jnp.float32)).astype(jnp.bfloat16)


def dot(a, b, dims=NN):
    return lax.dot_general(a, b, dims, preferred_element_type=jnp.float32)


def params(**kw):
    return pltpu.CompilerParams(vmem_limit_bytes=VMEM_LIMIT, **kw)


def look_up(src, rid, left, rel, span_len):
    count = src.shape[0]
    width = left.shape[1]

    def kernel(src, rid, left, rel, x, r):
        base = pl.program_id(0) * span_len

        @pl.loop(0, span_len // 16)
        def _(i):
            e0 = pl.multiple_of(i * 16, 16)
            for s in range(16):
                e = base + e0 + s
                x[pl.ds(e0 + s, 1), :] = left[pl.ds(src[e], 1), :]
                r[pl.ds(e0 + s, 1), :] = rel[pl.ds(rid[e], 1), :]

    scalars = pl.BlockSpec(memory_space=pltpu.SMEM)
    whole = pl.BlockSpec(memory_space=pltpu.VMEM)
    block = pl.BlockSpec((span_len, width), lambda b: (b, 0))
    return pl.pallas_call(
        kernel,
        grid=(count // span_len,),
        out_shape=[jax.ShapeDtypeStruct((count, width), jnp.float32)] * 2,
        in_specs=[scalars] * 2 + [whole] * 2,
        out_specs=[block] * 2,
        compiler_params=params(),
        cost_estimate=pl.CostEstimate(flops=0, bytes_accessed=10 * count * width, transcendentals=0),
        name="look_up",
    )(src, rid, left, rel)


def score_blocks(src, dst, rid, neg, x, r, right, left_rows, rel_rows, span_len):
    span_count, neg_count = neg.shape
    neg = neg.reshape(-1)
    count, width = x.shape
    tile = min(TILE, span_len)
    per = neg_count // span_len

    def kernel(src, dst, rid, neg, x, r, right, gl, grel, gy, gn, y, n, gx, gg):
        b = pl.program_id(0)

        def gather(i):
            e0 = pl.multiple_of(i * 8, 8)
            n0 = pl.multiple_of(i * 8 * per, 8 * per)
            for s in range(8):
                y[pl.ds(e0 + s, 1), :] = right[pl.ds(dst[b * span_len + e0 + s], 1), :]
                for k in range(per):
                    m = n0 + per * s + k
                    n[pl.ds(m, 1), :] = right[pl.ds(neg[b * neg_count + m], 1), :]

        def scatter(i):
            e0 = pl.multiple_of(i * 8, 8)
            for s in range(8):
                e = (b - 1) * span_len + e0 + s
                gl[pl.ds(src[e], 1), :] += gx[pl.ds(e0 + s, 1), :]
                grel[pl.ds(rid[e], 1), :] += gg[pl.ds(e0 + s, 1), :]

        @pl.when(b == 0)
        def _():
            gl[...] = jnp.zeros_like(gl)
            grel[...] = jnp.zeros_like(grel)

            @pl.loop(0, span_len // 8)
            def _(i):
                gather(i)

        @pl.when((b > 0) & (b < span_count))
        def _():
            @pl.loop(0, span_len // 8)
            def _(i):
                gather(i)
                scatter(i)

        @pl.when(b == span_count)
        def _():
            @pl.loop(0, span_len // 8)
            def _(i):
                scatter(i)

        @pl.when(b < span_count)
        def _():
            nh, nl = split(n[...])
            ncat = jnp.concatenate([nh, nl], axis=1)
            acc = jnp.zeros((2 * width, neg_count), jnp.float32)
            acc2 = jnp.zeros((width, neg_count), jnp.float32)
            for t in range(span_len // tile):
                rows = pl.ds(t * tile, tile)
                xv, rv, yv = x[rows, :], r[rows, :], y[rows, :]
                q = xv * rv
                pos = jnp.sum(q * yv, axis=1, keepdims=True)
                qh, ql = split(q)
                score = dot(jnp.concatenate([qh, ql], axis=1), jnp.concatenate([nh, nh], axis=1), NT) + dot(qh, nl, NT)
                w = jax.nn.sigmoid(score + (margin_gap - pos))
                total = jnp.sum(w, axis=1, keepdims=True) * (1.0 / neg_count)
                wh, wl = split(w)
                a = dot(wh, ncat)
                gq = (a[:, :width] + a[:, width:] + dot(wl, nh)) * (1.0 / neg_count) - total * yv
                gx[rows, :] = gq * rv
                gg[rows, :] = gq * xv
                gy[rows, :] = -total * q
                qth, qtl = split(q.T)
                acc += dot(jnp.concatenate([qth, qtl], axis=0), wh)
                acc2 += dot(qth, wl)
            gn[...] = ((acc[:width] + acc[width:] + acc2) * (1.0 / neg_count)).T

    scalars = pl.BlockSpec(memory_space=pltpu.SMEM)
    whole = pl.BlockSpec(memory_space=pltpu.VMEM)
    last = span_count - 1
    edge = pl.BlockSpec((span_len, width), lambda b: (jnp.minimum(b, last), 0))
    negs = pl.BlockSpec((neg_count, width), lambda b: (jnp.minimum(b, last), 0))
    edge_rows = pltpu.VMEM((span_len, width), jnp.float32)
    neg_rows = pltpu.VMEM((neg_count, width), jnp.float32)
    return pl.pallas_call(
        kernel,
        grid=(span_count + 1,),
        out_shape=[
            jax.ShapeDtypeStruct(shape, jnp.float32)
            for shape in ((left_rows, width), (rel_rows, width), (count, width), (neg.shape[0], width))
        ],
        in_specs=[scalars] * 4 + [edge] * 2 + [whole],
        out_specs=[whole] * 2 + [edge, negs],
        scratch_shapes=[edge_rows, neg_rows, edge_rows, edge_rows],
        compiler_params=params(),
        name="score_blocks",
    )(src, dst, rid, neg, x, r, right)


def scatter_right(dst, neg, gy, gn, part_rows, span_len):
    count, width = gy.shape
    span_count, neg_count = neg.shape
    neg = neg.reshape(-1)
    per = neg_count // span_len

    def kernel(dst, neg, gy, gn, out, odd, neg_even, neg_odd):
        b = pl.program_id(0)
        edge_sums, neg_sums = (out, odd), (neg_even, neg_odd)

        @pl.when(b == 0)
        def _():
            for a in edge_sums + neg_sums:
                a[...] = jnp.zeros_like(a)

        @pl.loop(0, span_len // 8)
        def _(i):
            e0 = pl.multiple_of(i * 8, 8)
            n0 = pl.multiple_of(i * 8 * per, 8 * per)
            for s in range(8):
                edge_sums[s % 2][pl.ds(dst[b * span_len + e0 + s], 1), :] += gy[pl.ds(e0 + s, 1), :]
                for k in range(per):
                    m = n0 + per * s + k
                    neg_sums[m_parity(s, k, per)][pl.ds(neg[b * neg_count + m], 1), :] += gn[pl.ds(m, 1), :]

        @pl.when(b == span_count - 1)
        def _():
            @pl.loop(0, part_rows // 256)
            def _(i):
                rows = pl.ds(pl.multiple_of(i * 256, 256), 256)
                out[rows, :] = (out[rows, :] + odd[rows, :]) + (neg_even[rows, :] + neg_odd[rows, :])

    scalars = pl.BlockSpec(memory_space=pltpu.SMEM)
    whole = pl.BlockSpec(memory_space=pltpu.VMEM)
    sums = pltpu.VMEM((part_rows, width), jnp.float32)
    return pl.pallas_call(
        kernel,
        grid=(span_count,),
        out_shape=jax.ShapeDtypeStruct((part_rows, width), jnp.float32),
        in_specs=[scalars] * 2
        + [pl.BlockSpec((span_len, width), lambda b: (b, 0)), pl.BlockSpec((neg_count, width), lambda b: (b, 0))],
        out_specs=whole,
        scratch_shapes=[sums] * 3,
        compiler_params=params(),
        cost_estimate=pl.CostEstimate(flops=0, bytes_accessed=40 * count * width, transcendentals=0),
        name="scatter_right",
    )(dst, neg, gy, gn)


def m_parity(s, k, per):
    return (per * s + k) % 2


def split_place(bucket):
    core = lax.rem(bucket, CORES)
    chip = lax.div(bucket, CORES)
    return {"core": core, "y": lax.rem(chip, SIDE), "z": lax.div(chip, SIDE), "x": lax.axis_index("dom")}


def peer_of(place, axis, by):
    size = SIZES[axis]
    spot = dict(place)
    spot[axis] = lax.rem(place[axis] + by, size)
    return {"bucket": (spot["z"] * SIDE + spot["y"]) * CORES + spot["core"], "dom": spot["x"]}


def sum_everywhere(grads):
    rows, width = grads.shape
    half = rows // len(ORDERS)

    def kernel(grad, out, *scratch):
        levels = len(ORDERS[0])
        parts = [scratch[k * levels : (k + 1) * levels] for k in range(len(ORDERS))]
        arrived = [scratch[(len(ORDERS) + k) * levels : (len(ORDERS) + k + 1) * levels] for k in range(len(ORDERS))]
        send_in, recv_in, send_out, recv_out = scratch[2 * len(ORDERS) * levels :]
        place = split_place(lax.axis_index("bucket"))
        barrier = pltpu.get_barrier_semaphore()
        greeted = 0
        for axis, size in SIZES.items():
            for by in range(1, size):
                pl.semaphore_signal(barrier, inc=1, device_id=peer_of(place, axis, by), device_id_type=MESH)
                greeted += 1
        pl.semaphore_wait(barrier, greeted)

        def copy(source, target, sends, recvs, k, level, by, axis):
            return pltpu.make_async_remote_copy(
                src_ref=source,
                dst_ref=target,
                send_sem=sends.at[k, level, by],
                recv_sem=recvs.at[k, level, by],
                device_id=peer_of(place, axis, by),
                device_id_type=MESH,
            )

        lows = [k * half for k in range(len(ORDERS))]
        starts = [[] for _ in ORDERS]
        for level in range(levels):
            copies = []
            for k, order in enumerate(ORDERS):
                axis = order[level]
                size = SIZES[axis]
                block = half // math.prod(SIZES[a] for a in order[: level + 1])
                source = grad if level == 0 else parts[k][level - 1]
                base = lows[k] if level == 0 else 0
                for by in range(1, size):
                    other = lax.rem(place[axis] + by, size)
                    c = copy(
                        source.at[pl.ds(pl.multiple_of(base + other * block, 8), block), :],
                        arrived[k][level].at[by - 1],
                        send_in, recv_in, k, level, by, axis,
                    )
                    c.start()
                    copies.append(c)
            for c in copies:
                c.wait()
            for k, order in enumerate(ORDERS):
                axis = order[level]
                size = SIZES[axis]
                block = half // math.prod(SIZES[a] for a in order[: level + 1])
                source = grad if level == 0 else parts[k][level - 1]
                base = lows[k] if level == 0 else 0
                own = source[pl.ds(pl.multiple_of(base + place[axis] * block, 8), block), :]
                for by in range(1, size):
                    own = own + arrived[k][level][by - 1]
                starts[k].append(place[axis] * block)
                if level < levels - 1:
                    parts[k][level][...] = own
                else:
                    first = lows[k] + sum(starts[k])
                    out[pl.ds(pl.multiple_of(first, 8), block), :] = own
        for level in reversed(range(levels)):
            copies = []
            for k, order in enumerate(ORDERS):
                axis = order[level]
                block = half // math.prod(SIZES[a] for a in order[: level + 1])
                first = lows[k] + sum(starts[k][: level + 1])
                where = out.at[pl.ds(pl.multiple_of(first, 8), block), :]
                for by in range(1, SIZES[axis]):
                    c = copy(where, where, send_out, recv_out, k, level, by, axis)
                    c.start()
                    copies.append(c)
            for c in copies:
                c.wait()

    parts, arrived = [], []
    for order in ORDERS:
        for level in range(len(order)):
            block = half // math.prod(SIZES[a] for a in order[: level + 1])
            parts.append(pltpu.VMEM((block, width), jnp.float32))
            arrived.append(pltpu.VMEM((SIZES[order[level]] - 1, block, width), jnp.float32))
    whole = pl.BlockSpec(memory_space=pltpu.VMEM)
    sems = pltpu.SemaphoreType.DMA((len(ORDERS), len(ORDERS[0]), SIDE))
    return pl.pallas_call(
        kernel,
        out_shape=jax.ShapeDtypeStruct(grads.shape, jnp.float32),
        in_specs=[whole],
        out_specs=whole,
        scratch_shapes=parts + arrived + [sems] * 4,
        compiler_params=pltpu.CompilerParams(
            collective_id=0, has_side_effects=True, vmem_limit_bytes=40 * 1024 * 1024
        ),
        cost_estimate=pl.CostEstimate(flops=2 * rows * width, bytes_accessed=40 * rows * width, transcendentals=0),
        name="relation_sums",
    )(grads)


def body(
    left_table,
    right_table,
    left_state,
    right_state,
    sources,
    targets,
    relation_ids,
    negatives,
    rotation,
    relations,
    relation_state,
):
    trainers = lax.axis_size("bucket")
    left_full = lax.all_gather(left_table, "dom", axis=0, tiled=True)
    right_rows = rotate(right_table, jnp.mod(rotation[0], trainers))
    right_full = lax.all_gather(right_rows, "dom", axis=0, tiled=True)
    span_len = sources.shape[0] // negatives.shape[0]
    part_rows, rel_rows = left_full.shape[0], relations.shape[0]
    x, r = look_up(sources, relation_ids, left_full, relations, span_len)
    left_grad, rel_grad, grad_y, grad_n = score_blocks(
        sources, targets, relation_ids, negatives, x, r, right_full, part_rows, rel_rows, span_len
    )
    left_share = lax.psum_scatter(left_grad, "dom", scatter_dimension=0, tiled=True)
    right_grad = scatter_right(targets, negatives, grad_y, grad_n, part_rows, span_len)
    right_grad, left_share = lax.optimization_barrier((right_grad, left_share))
    right_share = lax.psum_scatter(right_grad, "dom", scatter_dimension=0, tiled=True)
    right_share = rotate(right_share, jnp.mod(-rotation[0], trainers))
    new_left, new_left_acc = adagrad(left_table, left_state, left_share)
    new_right, new_right_acc = adagrad(right_table, right_state, right_share)
    rel_total = sum_everywhere(rel_grad)
    new_rel, new_rel_acc = adagrad(relations, relation_state, rel_total)
    return (new_left, new_right, new_left_acc, new_right_acc, new_rel, new_rel_acc)


def solution(mesh):
    both = ("bucket", "dom")
    return jax.shard_map(
        body,
        mesh=mesh,
        in_specs=(
            P(both, None),
            P(both, None),
            P(both),
            P(both),
            P(both),
            P(both),
            P(both),
            P(both, None),
            P(),
            P(),
            P(),
        ),
        out_specs=(P(both, None), P(both, None), P(both), P(both), P(), P()),
        check_vma=False,
    )
```

```python
import math

import jax
import jax.numpy as jnp
from jax import lax
from jax.experimental import pallas as pl
from jax.experimental.pallas import tpu as pltpu
from jax.sharding import PartitionSpec as P

learn_rate = 0.2
margin_gap = 1.0
TILE = 256
UNROLL = 32
SUMS = 2
NEG_SUMS = 4
VMEM_LIMIT = 60 * 1024 * 1024
MESH = pl.DeviceIdType.MESH
CORES, SIDE = 2, 4
SIZES = {"core": CORES, "y": SIDE, "z": SIDE, "x": SIDE}
ORDERS = (("core", "y", "z", "x"), ("core", "z", "y", "x"))
NT = (((1,), (1,)), ((), ()))
NN = (((1,), (0,)), ((), ()))


def adagrad(param, state, grad):
    new_state = state + jnp.mean(grad * grad, axis=-1)
    return (param - learn_rate * grad / jnp.sqrt(new_state)[:, None], new_state)


def rotate(array, amount):
    size = lax.axis_size("bucket")

    def move(by):
        if by == 0:
            return lambda a: a
        return lambda a: lax.ppermute(a, "bucket", [(i, (i - by) % size) for i in range(size)])

    return lax.switch(amount, [move(by) for by in range(size)], array)


def split(a):
    hi = a.astype(jnp.bfloat16)
    return hi, (a - hi.astype(jnp.float32)).astype(jnp.bfloat16)


def dot(a, b, dims=NN):
    return lax.dot_general(a, b, dims, preferred_element_type=jnp.float32)


def params(**kw):
    return pltpu.CompilerParams(vmem_limit_bytes=VMEM_LIMIT, **kw)


def look_up(src, rid, left, rel, span_len):
    count = src.shape[0]
    width = left.shape[1]

    def kernel(src, rid, left, rel, x, r):
        base = pl.program_id(0) * span_len

        @pl.loop(0, span_len // 16)
        def _(i):
            e0 = pl.multiple_of(i * 16, 16)
            for s in range(16):
                e = base + e0 + s
                x[pl.ds(e0 + s, 1), :] = left[pl.ds(src[e], 1), :]
                r[pl.ds(e0 + s, 1), :] = rel[pl.ds(rid[e], 1), :]

    scalars = pl.BlockSpec(memory_space=pltpu.SMEM)
    whole = pl.BlockSpec(memory_space=pltpu.VMEM)
    block = pl.BlockSpec((span_len, width), lambda b: (b, 0))
    return pl.pallas_call(
        kernel,
        grid=(count // span_len,),
        out_shape=[jax.ShapeDtypeStruct((count, width), jnp.float32)] * 2,
        in_specs=[scalars] * 2 + [whole] * 2,
        out_specs=[block] * 2,
        compiler_params=params(),
        cost_estimate=pl.CostEstimate(flops=0, bytes_accessed=10 * count * width, transcendentals=0),
        name="look_up",
    )(src, rid, left, rel)


def fold(sums):
    @pl.loop(0, sums[0].shape[0] // 256)
    def _(i):
        rows = pl.ds(pl.multiple_of(i * 256, 256), 256)
        total = sums[0][rows, :]
        for a in sums[1:]:
            total = total + a[rows, :]
        sums[0][rows, :] = total


def score_blocks(src, dst, rid, neg, x, r, right, left_rows, rel_rows, span_len):
    span_count, neg_count = neg.shape
    neg = neg.reshape(-1)
    count, width = x.shape
    tile = min(TILE, span_len)
    per = neg_count // span_len

    def kernel(src, dst, rid, neg, x, r, right_hbm, gl_hbm, grel_hbm, gy, gn, right, y, n, gx, gg, sems, *sums):
        b = pl.program_id(0)
        left_sums, rel_sums = sums[:SUMS], sums[SUMS:]

        def move_rows(i, gathers, scatters):
            e0 = pl.multiple_of(i * UNROLL, UNROLL)
            n0 = pl.multiple_of(i * UNROLL * per, UNROLL * per)
            now, before = b * span_len + e0, (b - 1) * span_len + e0
            for s in range(UNROLL):
                if scatters:
                    left_sums[s % SUMS][pl.ds(src[before + s], 1), :] += gx[pl.ds(e0 + s, 1), :]
                    rel_sums[s % SUMS][pl.ds(rid[before + s], 1), :] += gg[pl.ds(e0 + s, 1), :]
                if gathers:
                    y[pl.ds(e0 + s, 1), :] = right[pl.ds(dst[now + s], 1), :]
                    for m in range(per * s, per * s + per):
                        n[pl.ds(n0 + m, 1), :] = right[pl.ds(neg[b * neg_count + n0 + m], 1), :]

        def every_row(gathers, scatters):
            @pl.loop(0, span_len // UNROLL)
            def _(i):
                move_rows(i, gathers, scatters)

        @pl.when(b == 0)
        def _():
            copy = pltpu.make_async_copy(right_hbm, right, sems.at[0])
            copy.start()
            for a in left_sums + rel_sums:
                a[...] = jnp.zeros_like(a)
            copy.wait()

            every_row(True, False)

        @pl.when((b > 0) & (b < span_count))
        def _():
            every_row(True, True)

        @pl.when(b == span_count)
        def _():
            every_row(False, True)
            fold(left_sums)
            fold(rel_sums)
            left_copy = pltpu.make_async_copy(left_sums[0], gl_hbm, sems.at[0])
            rel_copy = pltpu.make_async_copy(rel_sums[0], grel_hbm, sems.at[1])
            left_copy.start()
            rel_copy.start()
            left_copy.wait()
            rel_copy.wait()

        @pl.when(b < span_count)
        def _():
            nh, nl = split(n[...])
            ncat = jnp.concatenate([nh, nl], axis=1)
            acc = jnp.zeros((2 * width, neg_count), jnp.float32)
            acc2 = jnp.zeros((width, neg_count), jnp.float32)
            for t in range(span_len // tile):
                rows = pl.ds(t * tile, tile)
                xv, rv, yv = x[rows, :], r[rows, :], y[rows, :]
                q = xv * rv
                pos = jnp.sum(q * yv, axis=1, keepdims=True)
                qh, ql = split(q)
                score = dot(jnp.concatenate([qh, ql], axis=1), jnp.concatenate([nh, nh], axis=1), NT) + dot(qh, nl, NT)
                w = jax.nn.sigmoid(score + (margin_gap - pos))
                total = jnp.sum(w, axis=1, keepdims=True) * (1.0 / neg_count)
                wh, wl = split(w)
                a = dot(wh, ncat)
                gq = (a[:, :width] + a[:, width:] + dot(wl, nh)) * (1.0 / neg_count) - total * yv
                gx[rows, :] = gq * rv
                gg[rows, :] = gq * xv
                gy[rows, :] = -total * q
                qth, qtl = split(q.T)
                acc += dot(jnp.concatenate([qth, qtl], axis=0), wh)
                acc2 += dot(qth, wl)
            gn[...] = ((acc[:width] + acc[width:] + acc2) * (1.0 / neg_count)).T

    scalars = pl.BlockSpec(memory_space=pltpu.SMEM)
    anywhere = pl.BlockSpec(memory_space=pl.ANY)
    last = span_count - 1
    edge = pl.BlockSpec((span_len, width), lambda b: (jnp.minimum(b, last), 0))
    negs = pl.BlockSpec((neg_count, width), lambda b: (jnp.minimum(b, last), 0))
    edge_rows = pltpu.VMEM((span_len, width), jnp.float32)
    neg_rows = pltpu.VMEM((neg_count, width), jnp.float32)
    return pl.pallas_call(
        kernel,
        grid=(span_count + 1,),
        out_shape=[
            jax.ShapeDtypeStruct(shape, jnp.float32)
            for shape in ((left_rows, width), (rel_rows, width), (count, width), (neg.shape[0], width))
        ],
        in_specs=[scalars] * 4 + [edge] * 2 + [anywhere],
        out_specs=[anywhere] * 2 + [edge, negs],
        scratch_shapes=[
            pltpu.VMEM(right.shape, jnp.float32),
            edge_rows,
            neg_rows,
            edge_rows,
            edge_rows,
            pltpu.SemaphoreType.DMA((2,)),
        ]
        + [pltpu.VMEM((left_rows, width), jnp.float32)] * SUMS
        + [pltpu.VMEM((rel_rows, width), jnp.float32)] * SUMS,
        compiler_params=params(),
        name="score_blocks",
    )(src, dst, rid, neg, x, r, right)


def scatter_right(dst, neg, gy, gn, part_rows, span_len):
    count, width = gy.shape
    span_count, neg_count = neg.shape
    neg = neg.reshape(-1)
    per = neg_count // span_len

    def kernel(dst, neg, gy_block, gn_block, out, gy, gn, *sums_sem):
        *sums, sem = sums_sem
        b = pl.program_id(0)
        edge_sums, neg_sums = sums[:2], sums[2:]
        gy[...] = gy_block[...]
        gn[...] = gn_block[...]

        @pl.when(b == 0)
        def _():
            for a in sums:
                a[...] = jnp.zeros_like(a)

        @pl.loop(0, span_len // UNROLL)
        def _(i):
            e0 = pl.multiple_of(i * UNROLL, UNROLL)
            n0 = pl.multiple_of(i * UNROLL * per, UNROLL * per)
            for s in range(UNROLL):
                edge_sums[s % 2][pl.ds(dst[b * span_len + e0 + s], 1), :] += gy[pl.ds(e0 + s, 1), :]
                for k in range(per):
                    m = n0 + per * s + k
                    neg_sums[(per * s + k) % len(neg_sums)][pl.ds(neg[b * neg_count + m], 1), :] += gn[pl.ds(m, 1), :]

        @pl.when(b == span_count - 1)
        def _():
            fold(sums)
            copy = pltpu.make_async_copy(sums[0], out, sem)
            copy.start()
            copy.wait()

    scalars = pl.BlockSpec(memory_space=pltpu.SMEM)
    sums = pltpu.VMEM((part_rows, width), jnp.float32)
    return pl.pallas_call(
        kernel,
        grid=(span_count,),
        out_shape=jax.ShapeDtypeStruct((part_rows, width), jnp.float32),
        in_specs=[scalars] * 2
        + [pl.BlockSpec((span_len, width), lambda b: (b, 0)), pl.BlockSpec((neg_count, width), lambda b: (b, 0))],
        out_specs=pl.BlockSpec(memory_space=pl.ANY),
        scratch_shapes=[pltpu.VMEM((span_len, width), jnp.float32), pltpu.VMEM((neg_count, width), jnp.float32)]
        + [sums] * (2 + NEG_SUMS)
        + [pltpu.SemaphoreType.DMA],
        compiler_params=params(),
        cost_estimate=pl.CostEstimate(flops=0, bytes_accessed=40 * count * width, transcendentals=0),
        name="scatter_right",
    )(dst, neg, gy, gn)


def split_place(bucket):
    core = lax.rem(bucket, CORES)
    chip = lax.div(bucket, CORES)
    return {"core": core, "y": lax.rem(chip, SIDE), "z": lax.div(chip, SIDE), "x": lax.axis_index("dom")}


def peer_of(place, axis, by):
    size = SIZES[axis]
    spot = dict(place)
    spot[axis] = lax.rem(place[axis] + by, size)
    return {"bucket": (spot["z"] * SIDE + spot["y"]) * CORES + spot["core"], "dom": spot["x"]}


def sum_everywhere(grads):
    rows, width = grads.shape
    half = rows // len(ORDERS)

    def kernel(grad, out, *scratch):
        levels = len(ORDERS[0])
        parts = [scratch[k * levels : (k + 1) * levels] for k in range(len(ORDERS))]
        arrived = [scratch[(len(ORDERS) + k) * levels : (len(ORDERS) + k + 1) * levels] for k in range(len(ORDERS))]
        send_in, recv_in, send_out, recv_out = scratch[2 * len(ORDERS) * levels :]
        place = split_place(lax.axis_index("bucket"))
        barrier = pltpu.get_barrier_semaphore()
        greeted = 0
        for axis, size in SIZES.items():
            for by in range(1, size):
                pl.semaphore_signal(barrier, inc=1, device_id=peer_of(place, axis, by), device_id_type=MESH)
                greeted += 1
        pl.semaphore_wait(barrier, greeted)

        def copy(source, target, sends, recvs, k, level, by, axis):
            return pltpu.make_async_remote_copy(
                src_ref=source,
                dst_ref=target,
                send_sem=sends.at[k, level, by],
                recv_sem=recvs.at[k, level, by],
                device_id=peer_of(place, axis, by),
                device_id_type=MESH,
            )

        lows = [k * half for k in range(len(ORDERS))]
        starts = [[] for _ in ORDERS]
        for level in range(levels):
            copies = []
            for k, order in enumerate(ORDERS):
                axis = order[level]
                size = SIZES[axis]
                block = half // math.prod(SIZES[a] for a in order[: level + 1])
                source = grad if level == 0 else parts[k][level - 1]
                base = lows[k] if level == 0 else 0
                for by in range(1, size):
                    other = lax.rem(place[axis] + by, size)
                    c = copy(
                        source.at[pl.ds(pl.multiple_of(base + other * block, 8), block), :],
                        arrived[k][level].at[by - 1],
                        send_in, recv_in, k, level, by, axis,
                    )
                    c.start()
                    copies.append(c)
            for c in copies:
                c.wait()
            for k, order in enumerate(ORDERS):
                axis = order[level]
                size = SIZES[axis]
                block = half // math.prod(SIZES[a] for a in order[: level + 1])
                source = grad if level == 0 else parts[k][level - 1]
                base = lows[k] if level == 0 else 0
                own = source[pl.ds(pl.multiple_of(base + place[axis] * block, 8), block), :]
                for by in range(1, size):
                    own = own + arrived[k][level][by - 1]
                starts[k].append(place[axis] * block)
                if level < levels - 1:
                    parts[k][level][...] = own
                else:
                    first = lows[k] + sum(starts[k])
                    out[pl.ds(pl.multiple_of(first, 8), block), :] = own
        for level in reversed(range(levels)):
            copies = []
            for k, order in enumerate(ORDERS):
                axis = order[level]
                block = half // math.prod(SIZES[a] for a in order[: level + 1])
                first = lows[k] + sum(starts[k][: level + 1])
                where = out.at[pl.ds(pl.multiple_of(first, 8), block), :]
                for by in range(1, SIZES[axis]):
                    c = copy(where, where, send_out, recv_out, k, level, by, axis)
                    c.start()
                    copies.append(c)
            for c in copies:
                c.wait()

    parts, arrived = [], []
    for order in ORDERS:
        for level in range(len(order)):
            block = half // math.prod(SIZES[a] for a in order[: level + 1])
            parts.append(pltpu.VMEM((block, width), jnp.float32))
            arrived.append(pltpu.VMEM((SIZES[order[level]] - 1, block, width), jnp.float32))
    whole = pl.BlockSpec(memory_space=pltpu.VMEM)
    sems = pltpu.SemaphoreType.DMA((len(ORDERS), len(ORDERS[0]), SIDE))
    return pl.pallas_call(
        kernel,
        out_shape=jax.ShapeDtypeStruct(grads.shape, jnp.float32),
        in_specs=[whole],
        out_specs=whole,
        scratch_shapes=parts + arrived + [sems] * 4,
        compiler_params=pltpu.CompilerParams(
            collective_id=0, has_side_effects=True, vmem_limit_bytes=40 * 1024 * 1024
        ),
        cost_estimate=pl.CostEstimate(flops=2 * rows * width, bytes_accessed=40 * rows * width, transcendentals=0),
        name="relation_sums",
    )(grads)


def body(
    left_table,
    right_table,
    left_state,
    right_state,
    sources,
    targets,
    relation_ids,
    negatives,
    rotation,
    relations,
    relation_state,
):
    trainers = lax.axis_size("bucket")
    left_full = lax.all_gather(left_table, "dom", axis=0, tiled=True)
    right_rows = rotate(right_table, jnp.mod(rotation[0], trainers))
    right_full = lax.all_gather(right_rows, "dom", axis=0, tiled=True)
    span_len = sources.shape[0] // negatives.shape[0]
    part_rows, rel_rows = left_full.shape[0], relations.shape[0]
    x, r = look_up(sources, relation_ids, left_full, relations, span_len)
    left_grad, rel_grad, grad_y, grad_n = score_blocks(
        sources, targets, relation_ids, negatives, x, r, right_full, part_rows, rel_rows, span_len
    )
    left_share = lax.psum_scatter(left_grad, "dom", scatter_dimension=0, tiled=True)
    right_grad = scatter_right(targets, negatives, grad_y, grad_n, part_rows, span_len)
    right_grad, left_share = lax.optimization_barrier((right_grad, left_share))
    right_share = lax.psum_scatter(right_grad, "dom", scatter_dimension=0, tiled=True)
    right_share = rotate(right_share, jnp.mod(-rotation[0], trainers))
    new_left, new_left_acc = adagrad(left_table, left_state, left_share)
    new_right, new_right_acc = adagrad(right_table, right_state, right_share)
    rel_total = sum_everywhere(rel_grad)
    new_rel, new_rel_acc = adagrad(relations, relation_state, rel_total)
    return (new_left, new_right, new_left_acc, new_right_acc, new_rel, new_rel_acc)


def solution(mesh):
    both = ("bucket", "dom")
    return jax.shard_map(
        body,
        mesh=mesh,
        in_specs=(
            P(both, None),
            P(both, None),
            P(both),
            P(both),
            P(both),
            P(both),
            P(both),
            P(both, None),
            P(),
            P(),
            P(),
        ),
        out_specs=(P(both, None), P(both, None), P(both), P(both), P(), P()),
        check_vma=False,
    )
```

```python
import math

import jax
import jax.numpy as jnp
from jax import lax
from jax.experimental import pallas as pl
from jax.experimental.pallas import tpu as pltpu
from jax.sharding import PartitionSpec as P

learn_rate = 0.2
margin_gap = 1.0
TILE = 256
UNROLL = 32
SUMS = 2
NEG_SUMS = 4
VMEM_LIMIT = 60 * 1024 * 1024
MESH = pl.DeviceIdType.MESH
CORES, SIDE = 2, 4
SIZES = {"core": CORES, "y": SIDE, "z": SIDE, "x": SIDE}
ORDERS = (("core", "y", "z", "x"), ("core", "z", "y", "x"))
RELAYED = 1
NT = (((1,), (1,)), ((), ()))
NN = (((1,), (0,)), ((), ()))


def adagrad(param, state, grad):
    new_state = state + jnp.mean(grad * grad, axis=-1)
    return (param - learn_rate * grad / jnp.sqrt(new_state)[:, None], new_state)


def shifted(array, by):
    size = lax.axis_size("bucket")
    if by == 0:
        return array
    return lax.ppermute(array, "bucket", [(i, (i - by) % size) for i in range(size)])


def rotate(array, amount):
    return lax.switch(amount, [lambda a, by=by: shifted(a, by) for by in range(lax.axis_size("bucket"))], array)


def split(a):
    hi = a.astype(jnp.bfloat16)
    return hi, (a - hi.astype(jnp.float32)).astype(jnp.bfloat16)


def dot(a, b, dims=NN):
    return lax.dot_general(a, b, dims, preferred_element_type=jnp.float32)


def params(**kw):
    return pltpu.CompilerParams(vmem_limit_bytes=VMEM_LIMIT, **kw)


def look_up(src, rid, left, rel, span_len):
    count = src.shape[0]
    width = left.shape[1]

    def kernel(src, rid, left, rel, x, r):
        base = pl.program_id(0) * span_len

        @pl.loop(0, span_len // 16)
        def _(i):
            e0 = pl.multiple_of(i * 16, 16)
            for s in range(16):
                e = base + e0 + s
                x[pl.ds(e0 + s, 1), :] = left[pl.ds(src[e], 1), :]
                r[pl.ds(e0 + s, 1), :] = rel[pl.ds(rid[e], 1), :]

    scalars = pl.BlockSpec(memory_space=pltpu.SMEM)
    whole = pl.BlockSpec(memory_space=pltpu.VMEM)
    block = pl.BlockSpec((span_len, width), lambda b: (b, 0))
    return pl.pallas_call(
        kernel,
        grid=(count // span_len,),
        out_shape=[jax.ShapeDtypeStruct((count, width), jnp.float32)] * 2,
        in_specs=[scalars] * 2 + [whole] * 2,
        out_specs=[block] * 2,
        compiler_params=params(),
        cost_estimate=pl.CostEstimate(flops=0, bytes_accessed=10 * count * width, transcendentals=0),
        name="look_up",
    )(src, rid, left, rel)


def fold(sums):
    @pl.loop(0, sums[0].shape[0] // 256)
    def _(i):
        rows = pl.ds(pl.multiple_of(i * 256, 256), 256)
        total = sums[0][rows, :]
        for a in sums[1:]:
            total = total + a[rows, :]
        sums[0][rows, :] = total


def score_blocks(src, dst, rid, neg, x, r, right, left_rows, rel_rows, span_len):
    span_count, neg_count = neg.shape
    neg = neg.reshape(-1)
    count, width = x.shape
    tile = min(TILE, span_len)
    per = neg_count // span_len

    def kernel(src, dst, rid, neg, x, r, right_hbm, gl_hbm, grel_hbm, gy, gn, right, y, n, gx, gg, sems, *sums):
        b = pl.program_id(0)
        left_sums, rel_sums = sums[:SUMS], sums[SUMS:]

        def move_rows(i, gathers, scatters):
            e0 = pl.multiple_of(i * UNROLL, UNROLL)
            n0 = pl.multiple_of(i * UNROLL * per, UNROLL * per)
            now, before = b * span_len + e0, (b - 1) * span_len + e0
            for s in range(UNROLL):
                if scatters:
                    left_sums[s % SUMS][pl.ds(src[before + s], 1), :] += gx[pl.ds(e0 + s, 1), :]
                    rel_sums[s % SUMS][pl.ds(rid[before + s], 1), :] += gg[pl.ds(e0 + s, 1), :]
                if gathers:
                    y[pl.ds(e0 + s, 1), :] = right[pl.ds(dst[now + s], 1), :]
                    for m in range(per * s, per * s + per):
                        n[pl.ds(n0 + m, 1), :] = right[pl.ds(neg[b * neg_count + n0 + m], 1), :]

        def every_row(gathers, scatters):
            @pl.loop(0, span_len // UNROLL)
            def _(i):
                move_rows(i, gathers, scatters)

        @pl.when(b == 0)
        def _():
            copy = pltpu.make_async_copy(right_hbm, right, sems.at[0])
            copy.start()
            for a in left_sums + rel_sums:
                a[...] = jnp.zeros_like(a)
            copy.wait()

            every_row(True, False)

        @pl.when((b > 0) & (b < span_count))
        def _():
            every_row(True, True)

        @pl.when(b == span_count)
        def _():
            every_row(False, True)
            fold(left_sums)
            fold(rel_sums)
            left_copy = pltpu.make_async_copy(left_sums[0], gl_hbm, sems.at[0])
            rel_copy = pltpu.make_async_copy(rel_sums[0], grel_hbm, sems.at[1])
            left_copy.start()
            rel_copy.start()
            left_copy.wait()
            rel_copy.wait()

        @pl.when(b < span_count)
        def _():
            nh, nl = split(n[...])
            ncat = jnp.concatenate([nh, nl], axis=1)
            acc = jnp.zeros((2 * width, neg_count), jnp.float32)
            acc2 = jnp.zeros((width, neg_count), jnp.float32)
            for t in range(span_len // tile):
                rows = pl.ds(t * tile, tile)
                xv, rv, yv = x[rows, :], r[rows, :], y[rows, :]
                q = xv * rv
                pos = jnp.sum(q * yv, axis=1, keepdims=True)
                qh, ql = split(q)
                score = dot(jnp.concatenate([qh, ql], axis=1), jnp.concatenate([nh, nh], axis=1), NT) + dot(qh, nl, NT)
                w = jax.nn.sigmoid(score + (margin_gap - pos))
                total = jnp.sum(w, axis=1, keepdims=True) * (1.0 / neg_count)
                wh, wl = split(w)
                a = dot(wh, ncat)
                gq = (a[:, :width] + a[:, width:] + dot(wl, nh)) * (1.0 / neg_count) - total * yv
                gx[rows, :] = gq * rv
                gg[rows, :] = gq * xv
                gy[rows, :] = -total * q
                qth, qtl = split(q.T)
                acc += dot(jnp.concatenate([qth, qtl], axis=0), wh)
                acc2 += dot(qth, wl)
            gn[...] = ((acc[:width] + acc[width:] + acc2) * (1.0 / neg_count)).T

    scalars = pl.BlockSpec(memory_space=pltpu.SMEM)
    anywhere = pl.BlockSpec(memory_space=pl.ANY)
    last = span_count - 1
    edge = pl.BlockSpec((span_len, width), lambda b: (jnp.minimum(b, last), 0))
    negs = pl.BlockSpec((neg_count, width), lambda b: (jnp.minimum(b, last), 0))
    edge_rows = pltpu.VMEM((span_len, width), jnp.float32)
    neg_rows = pltpu.VMEM((neg_count, width), jnp.float32)
    return pl.pallas_call(
        kernel,
        grid=(span_count + 1,),
        out_shape=[
            jax.ShapeDtypeStruct(shape, jnp.float32)
            for shape in ((left_rows, width), (rel_rows, width), (count, width), (neg.shape[0], width))
        ],
        in_specs=[scalars] * 4 + [edge] * 2 + [anywhere],
        out_specs=[anywhere] * 2 + [edge, negs],
        scratch_shapes=[
            pltpu.VMEM(right.shape, jnp.float32),
            edge_rows,
            neg_rows,
            edge_rows,
            edge_rows,
            pltpu.SemaphoreType.DMA((2,)),
        ]
        + [pltpu.VMEM((left_rows, width), jnp.float32)] * SUMS
        + [pltpu.VMEM((rel_rows, width), jnp.float32)] * SUMS,
        compiler_params=params(),
        name="score_blocks",
    )(src, dst, rid, neg, x, r, right)


def scatter_right(dst, neg, gy, gn, part_rows, span_len):
    count, width = gy.shape
    span_count, neg_count = neg.shape
    per = neg_count // span_len
    draws = [neg[:, k * span_len : (k + 1) * span_len].reshape(-1) for k in range(per)]

    def kernel(dst, *rest):
        draws, (gy_block, gn_block, out, gy, gn, sem), sums = rest[:per], rest[per : per + 6], rest[per + 6 :]
        b = pl.program_id(0)
        edge_sums, neg_sums = sums[:2], sums[2:]
        gy[...] = gy_block[...]
        gn[...] = gn_block[...]

        @pl.when(b == 0)
        def _():
            for a in sums:
                a[...] = jnp.zeros_like(a)

        @pl.loop(0, span_len // UNROLL)
        def _(i):
            e0 = pl.multiple_of(i * UNROLL, UNROLL)
            at = b * span_len + e0
            for s in range(UNROLL):
                edge_sums[s % 2][pl.ds(dst[at + s], 1), :] += gy[pl.ds(e0 + s, 1), :]
                for k in range(per):
                    row = draws[k][at + s]
                    neg_sums[(per * s + k) % len(neg_sums)][pl.ds(row, 1), :] += gn[pl.ds(k * span_len + e0 + s, 1), :]

        @pl.when(b == span_count - 1)
        def _():
            fold(sums)
            copy = pltpu.make_async_copy(sums[0], out, sem)
            copy.start()
            copy.wait()

    scalars = pl.BlockSpec(memory_space=pltpu.SMEM)
    sums = pltpu.VMEM((part_rows, width), jnp.float32)
    return pl.pallas_call(
        kernel,
        grid=(span_count,),
        out_shape=jax.ShapeDtypeStruct((part_rows, width), jnp.float32),
        in_specs=[scalars] * (1 + per)
        + [pl.BlockSpec((span_len, width), lambda b: (b, 0)), pl.BlockSpec((neg_count, width), lambda b: (b, 0))],
        out_specs=pl.BlockSpec(memory_space=pl.ANY),
        scratch_shapes=[pltpu.VMEM((span_len, width), jnp.float32), pltpu.VMEM((neg_count, width), jnp.float32)]
        + [pltpu.SemaphoreType.DMA]
        + [sums] * (2 + NEG_SUMS),
        compiler_params=params(),
        cost_estimate=pl.CostEstimate(flops=0, bytes_accessed=40 * count * width, transcendentals=0),
        name="scatter_right",
    )(dst, *draws, gy, gn)


def split_place(bucket):
    core = lax.rem(bucket, CORES)
    chip = lax.div(bucket, CORES)
    return {"core": core, "y": lax.rem(chip, SIDE), "z": lax.div(chip, SIDE), "x": lax.axis_index("dom")}


def peer_of(place, axis, by):
    size = SIZES[axis]
    spot = dict(place)
    spot[axis] = lax.rem(place[axis] + by, size)
    return {"bucket": (spot["z"] * SIDE + spot["y"]) * CORES + spot["core"], "dom": spot["x"]}


def sum_everywhere(grads):
    rows, width = grads.shape
    half = rows // len(ORDERS)

    def kernel(grad, out, *scratch):
        levels = len(ORDERS[0])
        parts = [scratch[k * levels : (k + 1) * levels] for k in range(len(ORDERS))]
        arrived = [scratch[(len(ORDERS) + k) * levels : (len(ORDERS) + k + 1) * levels] for k in range(len(ORDERS))]
        rest = scratch[2 * len(ORDERS) * levels :]
        send_in, recv_in, send_out, recv_out, send_on, recv_on = rest[:6]
        staged = rest[6:]
        place = split_place(lax.axis_index("bucket"))
        barrier = pltpu.get_barrier_semaphore()
        greeted = 0
        for axis, size in SIZES.items():
            for by in range(1, size):
                pl.semaphore_signal(barrier, inc=1, device_id=peer_of(place, axis, by), device_id_type=MESH)
                greeted += 1
        pl.semaphore_wait(barrier, greeted)

        def copy(source, target, sends, recvs, k, level, by, axis):
            return pltpu.make_async_remote_copy(
                src_ref=source,
                dst_ref=target,
                send_sem=sends.at[k, level, by],
                recv_sem=recvs.at[k, level, by],
                device_id=peer_of(place, axis, by),
                device_id_type=MESH,
            )

        def pass_on(source, target, k, index, by, axis):
            return pltpu.make_async_remote_copy(
                src_ref=source,
                dst_ref=target,
                send_sem=send_on.at[k, index],
                recv_sem=recv_on.at[k, index],
                device_id=peer_of(place, axis, by),
                device_id_type=MESH,
            )

        lows = [k * half for k in range(len(ORDERS))]
        starts = [[] for _ in ORDERS]
        for level in range(levels):
            copies = []
            if level == RELAYED:
                relays = []
                for k, order in enumerate(ORDERS):
                    axis = order[level]
                    source, slots = parts[k][level - 1], arrived[k][level]
                    rows = slots.shape[1] // 2

                    def piece(by, upper, axis=axis, rows=rows):
                        at = lax.rem(place[axis] + by, SIDE) * (2 * rows) + upper * rows
                        return pl.ds(pl.multiple_of(at, 8), rows)

                    low, high = pl.ds(0, rows), pl.ds(rows, rows)
                    to_up = pass_on(source.at[piece(2, 0), :], slots.at[2, low, :], k, 0, 1, axis)
                    to_down = pass_on(source.at[piece(2, 1), :], slots.at[2, high, :], k, 1, SIDE - 1, axis)
                    plain_up = pass_on(source.at[piece(1, 1), :], slots.at[0, high, :], k, 2, 1, axis)
                    plain_down = pass_on(source.at[piece(SIDE - 1, 0), :], slots.at[1, low, :], k, 3, SIDE - 1, axis)
                    for c in (to_up, to_down, plain_up, plain_down):
                        c.start()
                    relays.append((k, axis, source, slots, piece, low, high, to_up, to_down))
                    copies += [plain_up, plain_down]
                for k, axis, source, slots, piece, low, high, to_up, to_down in relays:
                    to_up.wait()
                    staged[k][0] = source[piece(1, 0), :] + slots[2, low, :]
                    sum_up = pass_on(staged[k].at[0], slots.at[0, low, :], k, 4, 1, axis)
                    sum_up.start()
                    to_down.wait()
                    staged[k][1] = source[piece(SIDE - 1, 1), :] + slots[2, high, :]
                    sum_down = pass_on(staged[k].at[1], slots.at[1, high, :], k, 5, SIDE - 1, axis)
                    sum_down.start()
                    copies += [sum_up, sum_down]
            for k, order in enumerate(ORDERS):
                axis = order[level]
                size = SIZES[axis]
                block = half // math.prod(SIZES[a] for a in order[: level + 1])
                source = grad if level == 0 else parts[k][level - 1]
                base = lows[k] if level == 0 else 0
                for by in range(1, 1 if level == RELAYED else size):
                    other = lax.rem(place[axis] + by, size)
                    c = copy(
                        source.at[pl.ds(pl.multiple_of(base + other * block, 8), block), :],
                        arrived[k][level].at[by - 1],
                        send_in, recv_in, k, level, by, axis,
                    )
                    c.start()
                    copies.append(c)
            for c in copies:
                c.wait()
            for k, order in enumerate(ORDERS):
                axis = order[level]
                size = SIZES[axis]
                block = half // math.prod(SIZES[a] for a in order[: level + 1])
                source = grad if level == 0 else parts[k][level - 1]
                base = lows[k] if level == 0 else 0
                own = source[pl.ds(pl.multiple_of(base + place[axis] * block, 8), block), :]
                for by in range(1, SIDE - 1 if level == RELAYED else size):
                    own = own + arrived[k][level][by - 1]
                starts[k].append(place[axis] * block)
                if level < levels - 1:
                    parts[k][level][...] = own
                else:
                    first = lows[k] + sum(starts[k])
                    out[pl.ds(pl.multiple_of(first, 8), block), :] = own
        for level in reversed(range(levels)):
            copies = []
            if level == RELAYED:
                relays = []
                for k, order in enumerate(ORDERS):
                    axis = order[level]
                    block = half // math.prod(SIZES[a] for a in order[: level + 1])
                    base = lows[k] + sum(starts[k][:level])

                    def piece(by, skip, rows, axis=axis, block=block, base=base):
                        at = base + lax.rem(place[axis] + by, SIDE) * block + skip
                        return out.at[pl.ds(pl.multiple_of(at, 8), rows), :]

                    own = piece(0, 0, block)
                    to_up = pass_on(own, own, k, 6, 1, axis)
                    to_down = pass_on(own, own, k, 7, SIDE - 1, axis)
                    to_up.start()
                    to_down.start()
                    relays.append((k, axis, block // 2, piece, to_up, to_down))
                for k, axis, rows, piece, to_up, to_down in relays:
                    to_up.wait()
                    below = piece(SIDE - 1, 0, rows)
                    on_up = pass_on(below, below, k, 8, 1, axis)
                    on_up.start()
                    to_down.wait()
                    above = piece(1, rows, rows)
                    on_down = pass_on(above, above, k, 9, SIDE - 1, axis)
                    on_down.start()
                    copies += [on_up, on_down]
            for k, order in enumerate(ORDERS if level != RELAYED else ()):
                axis = order[level]
                block = half // math.prod(SIZES[a] for a in order[: level + 1])
                first = lows[k] + sum(starts[k][: level + 1])
                where = out.at[pl.ds(pl.multiple_of(first, 8), block), :]
                for by in range(1, SIZES[axis]):
                    c = copy(where, where, send_out, recv_out, k, level, by, axis)
                    c.start()
                    copies.append(c)
            for c in copies:
                c.wait()

    parts, arrived = [], []
    for order in ORDERS:
        for level in range(len(order)):
            block = half // math.prod(SIZES[a] for a in order[: level + 1])
            parts.append(pltpu.VMEM((block, width), jnp.float32))
            arrived.append(pltpu.VMEM((SIZES[order[level]] - 1, block, width), jnp.float32))
    rows = half // math.prod(SIZES[a] for a in ORDERS[0][: RELAYED + 1]) // 2
    staged = [pltpu.VMEM((2, rows, width), jnp.float32) for _ in ORDERS]
    on_sems = pltpu.SemaphoreType.DMA((len(ORDERS), 10))
    whole = pl.BlockSpec(memory_space=pltpu.VMEM)
    sems = pltpu.SemaphoreType.DMA((len(ORDERS), len(ORDERS[0]), SIDE))
    return pl.pallas_call(
        kernel,
        out_shape=jax.ShapeDtypeStruct(grads.shape, jnp.float32),
        in_specs=[whole],
        out_specs=whole,
        scratch_shapes=parts + arrived + [sems] * 4 + [on_sems] * 2 + staged,
        compiler_params=pltpu.CompilerParams(
            collective_id=0, has_side_effects=True, vmem_limit_bytes=40 * 1024 * 1024
        ),
        cost_estimate=pl.CostEstimate(flops=2 * half * width, bytes_accessed=80 * half * width, transcendentals=0),
        name="relation_sums",
    )(grads)


def body(
    left_table,
    right_table,
    left_state,
    right_state,
    sources,
    targets,
    relation_ids,
    negatives,
    rotation,
    relations,
    relation_state,
):
    trainers = lax.axis_size("bucket")
    left_full = lax.all_gather(left_table, "dom", axis=0, tiled=True)
    right_rows = rotate(right_table, jnp.mod(rotation[0], trainers))
    right_full = lax.all_gather(right_rows, "dom", axis=0, tiled=True)
    span_len = sources.shape[0] // negatives.shape[0]
    part_rows, rel_rows = left_full.shape[0], relations.shape[0]
    x, r = look_up(sources, relation_ids, left_full, relations, span_len)
    left_grad, rel_grad, grad_y, grad_n = score_blocks(
        sources, targets, relation_ids, negatives, x, r, right_full, part_rows, rel_rows, span_len
    )
    left_share = lax.psum_scatter(left_grad, "dom", scatter_dimension=0, tiled=True)
    right_grad = scatter_right(targets, negatives, grad_y, grad_n, part_rows, span_len)
    right_grad, left_share = lax.optimization_barrier((right_grad, left_share))
    right_share = lax.psum_scatter(right_grad, "dom", scatter_dimension=0, tiled=True)
    rel_total = sum_everywhere(rel_grad)

    def close(by):
        def branch(right_share, left_share, rel_total):
            moved = shifted(right_share, by)
            return moved, adagrad(left_table, left_state, left_share), adagrad(relations, relation_state, rel_total)

        return branch

    backward = jnp.mod(-rotation[0], trainers)
    right_share, left_new, rel_new = lax.switch(
        backward, [close(by) for by in range(trainers)], right_share, left_share, rel_total
    )
    new_right, new_right_acc = adagrad(right_table, right_state, right_share)
    (new_left, new_left_acc), (new_rel, new_rel_acc) = left_new, rel_new
    return (new_left, new_right, new_left_acc, new_right_acc, new_rel, new_rel_acc)


def solution(mesh):
    both = ("bucket", "dom")
    return jax.shard_map(
        body,
        mesh=mesh,
        in_specs=(
            P(both, None),
            P(both, None),
            P(both),
            P(both),
            P(both),
            P(both),
            P(both),
            P(both, None),
            P(),
            P(),
            P(),
        ),
        out_specs=(P(both, None), P(both, None), P(both), P(both), P(), P()),
        check_vma=False,
    )
```

```python
import math

import jax
import jax.numpy as jnp
from jax import lax
from jax.experimental import pallas as pl
from jax.experimental.pallas import tpu as pltpu
from jax.sharding import PartitionSpec as P

learn_rate = 0.2
margin_gap = 1.0
TILE = 256
UNROLL = 32
SUMS = 2
NEG_SUMS = 4
VMEM_LIMIT = 60 * 1024 * 1024
MESH = pl.DeviceIdType.MESH
CORES, SIDE = 2, 4
SIZES = {"core": CORES, "y": SIDE, "z": SIDE, "x": SIDE}
ORDERS = ((("core",), ("y",), ("z", "x")), (("core",), ("z",), ("y", "x")))
NT = (((1,), (1,)), ((), ()))
NN = (((1,), (0,)), ((), ()))


def adagrad(param, state, grad):
    new_state = state + jnp.mean(grad * grad, axis=-1)
    return (param - learn_rate * grad / jnp.sqrt(new_state)[:, None], new_state)


def rotate(array, amount):
    size = lax.axis_size("bucket")

    def move(by):
        if by == 0:
            return lambda a: a
        return lambda a: lax.ppermute(a, "bucket", [(i, (i - by) % size) for i in range(size)])

    return lax.switch(amount, [move(by) for by in range(size)], array)


def split(a):
    hi = a.astype(jnp.bfloat16)
    return hi, (a - hi.astype(jnp.float32)).astype(jnp.bfloat16)


def dot(a, b, dims=NN):
    return lax.dot_general(a, b, dims, preferred_element_type=jnp.float32)


def params(**kw):
    return pltpu.CompilerParams(vmem_limit_bytes=VMEM_LIMIT, **kw)


def look_up(src, rid, left, rel, span_len):
    count = src.shape[0]
    width = left.shape[1]

    def kernel(src, rid, left, rel, x, r):
        base = pl.program_id(0) * span_len

        @pl.loop(0, span_len // 16)
        def _(i):
            e0 = pl.multiple_of(i * 16, 16)
            for s in range(16):
                e = base + e0 + s
                x[pl.ds(e0 + s, 1), :] = left[pl.ds(src[e], 1), :]
                r[pl.ds(e0 + s, 1), :] = rel[pl.ds(rid[e], 1), :]

    scalars = pl.BlockSpec(memory_space=pltpu.SMEM)
    whole = pl.BlockSpec(memory_space=pltpu.VMEM)
    block = pl.BlockSpec((span_len, width), lambda b: (b, 0))
    return pl.pallas_call(
        kernel,
        grid=(count // span_len,),
        out_shape=[jax.ShapeDtypeStruct((count, width), jnp.float32)] * 2,
        in_specs=[scalars] * 2 + [whole] * 2,
        out_specs=[block] * 2,
        compiler_params=params(),
        cost_estimate=pl.CostEstimate(flops=0, bytes_accessed=10 * count * width, transcendentals=0),
        name="look_up",
    )(src, rid, left, rel)


def fold(sums):
    @pl.loop(0, sums[0].shape[0] // 256)
    def _(i):
        rows = pl.ds(pl.multiple_of(i * 256, 256), 256)
        total = sums[0][rows, :]
        for a in sums[1:]:
            total = total + a[rows, :]
        sums[0][rows, :] = total


def score_blocks(src, dst, rid, neg, x, r, right, left_rows, rel_rows, span_len):
    span_count, neg_count = neg.shape
    count, width = x.shape
    tile = min(TILE, span_len)
    per = neg_count // span_len
    draws = [neg[:, k * span_len : (k + 1) * span_len].reshape(-1) for k in range(per)]
    src, rid = jnp.roll(src, span_len), jnp.roll(rid, span_len)

    def kernel(src, dst, rid, *rest):
        draws, (x, r, right_hbm, gl_hbm, grel_hbm, gy, gn, right, y, n, gx, gg, sems), sums = (
            rest[:per],
            rest[per : per + 13],
            rest[per + 13 :],
        )
        b = pl.program_id(0)
        left_sums, rel_sums = sums[:SUMS], sums[SUMS:]

        def move_rows(i, gathers, scatters):
            e0 = pl.multiple_of(i * UNROLL, UNROLL)
            at = (b if gathers else 0) * span_len + e0
            for s in range(UNROLL):
                if scatters:
                    left_sums[s % SUMS][pl.ds(src[at + s], 1), :] += gx[pl.ds(e0 + s, 1), :]
                    rel_sums[s % SUMS][pl.ds(rid[at + s], 1), :] += gg[pl.ds(e0 + s, 1), :]
                if gathers:
                    y[pl.ds(e0 + s, 1), :] = right[pl.ds(dst[at + s], 1), :]
                    for k in range(per):
                        n[pl.ds(k * span_len + e0 + s, 1), :] = right[pl.ds(draws[k][at + s], 1), :]

        def every_row(gathers, scatters):
            @pl.loop(0, span_len // UNROLL)
            def _(i):
                move_rows(i, gathers, scatters)

        @pl.when(b == 0)
        def _():
            copy = pltpu.make_async_copy(right_hbm, right, sems.at[0])
            copy.start()
            for a in left_sums + rel_sums:
                a[...] = jnp.zeros_like(a)
            copy.wait()

            every_row(True, False)

        @pl.when((b > 0) & (b < span_count))
        def _():
            every_row(True, True)

        @pl.when(b == span_count)
        def _():
            every_row(False, True)
            fold(left_sums)
            fold(rel_sums)
            left_copy = pltpu.make_async_copy(left_sums[0], gl_hbm, sems.at[0])
            rel_copy = pltpu.make_async_copy(rel_sums[0], grel_hbm, sems.at[1])
            left_copy.start()
            rel_copy.start()
            left_copy.wait()
            rel_copy.wait()

        @pl.when(b < span_count)
        def _():
            nh, nl = split(n[...])
            ncat = jnp.concatenate([nh, nl], axis=1)
            acc = jnp.zeros((2 * width, neg_count), jnp.float32)
            acc2 = jnp.zeros((width, neg_count), jnp.float32)
            for t in range(span_len // tile):
                rows = pl.ds(t * tile, tile)
                xv, rv, yv = x[rows, :], r[rows, :], y[rows, :]
                q = xv * rv
                pos = jnp.sum(q * yv, axis=1, keepdims=True)
                qh, ql = split(q)
                score = dot(jnp.concatenate([qh, ql], axis=1), jnp.concatenate([nh, nh], axis=1), NT) + dot(qh, nl, NT)
                w = jax.nn.sigmoid(score + (margin_gap - pos))
                total = jnp.sum(w, axis=1, keepdims=True) * (1.0 / neg_count)
                wh, wl = split(w)
                a = dot(wh, ncat)
                gq = (a[:, :width] + a[:, width:] + dot(wl, nh)) * (1.0 / neg_count) - total * yv
                gx[rows, :] = gq * rv
                gg[rows, :] = gq * xv
                gy[rows, :] = -total * q
                qth, qtl = split(q.T)
                acc += dot(jnp.concatenate([qth, qtl], axis=0), wh)
                acc2 += dot(qth, wl)
            gn[...] = ((acc[:width] + acc[width:] + acc2) * (1.0 / neg_count)).T

    scalars = pl.BlockSpec(memory_space=pltpu.SMEM)
    anywhere = pl.BlockSpec(memory_space=pl.ANY)
    last = span_count - 1
    edge = pl.BlockSpec((span_len, width), lambda b: (jnp.minimum(b, last), 0))
    negs = pl.BlockSpec((neg_count, width), lambda b: (jnp.minimum(b, last), 0))
    edge_rows = pltpu.VMEM((span_len, width), jnp.float32)
    neg_rows = pltpu.VMEM((neg_count, width), jnp.float32)
    return pl.pallas_call(
        kernel,
        grid=(span_count + 1,),
        out_shape=[
            jax.ShapeDtypeStruct(shape, jnp.float32)
            for shape in ((left_rows, width), (rel_rows, width), (count, width), (span_count * neg_count, width))
        ],
        in_specs=[scalars] * (3 + per) + [edge] * 2 + [anywhere],
        out_specs=[anywhere] * 2 + [edge, negs],
        scratch_shapes=[
            pltpu.VMEM(right.shape, jnp.float32),
            edge_rows,
            neg_rows,
            edge_rows,
            edge_rows,
            pltpu.SemaphoreType.DMA((2,)),
        ]
        + [pltpu.VMEM((left_rows, width), jnp.float32)] * SUMS
        + [pltpu.VMEM((rel_rows, width), jnp.float32)] * SUMS,
        compiler_params=params(),
        name="score_blocks",
    )(src, dst, rid, *draws, x, r, right)


def scatter_right(dst, neg, gy, gn, part_rows, span_len):
    count, width = gy.shape
    span_count, neg_count = neg.shape
    per = neg_count // span_len
    draws = [neg[:, k * span_len : (k + 1) * span_len].reshape(-1) for k in range(per)]

    def kernel(dst, *rest):
        draws, (gy_block, gn_block, out, gy, gn, sem), sums = rest[:per], rest[per : per + 6], rest[per + 6 :]
        b = pl.program_id(0)
        edge_sums, neg_sums = sums[:2], sums[2:]
        gy[...] = gy_block[...]
        gn[...] = gn_block[...]

        @pl.when(b == 0)
        def _():
            for a in sums:
                a[...] = jnp.zeros_like(a)

        @pl.loop(0, span_len // UNROLL)
        def _(i):
            e0 = pl.multiple_of(i * UNROLL, UNROLL)
            at = b * span_len + e0
            for s in range(UNROLL):
                edge_sums[s % 2][pl.ds(dst[at + s], 1), :] += gy[pl.ds(e0 + s, 1), :]
                for k in range(per):
                    row = draws[k][at + s]
                    neg_sums[(per * s + k) % len(neg_sums)][pl.ds(row, 1), :] += gn[pl.ds(k * span_len + e0 + s, 1), :]

        @pl.when(b == span_count - 1)
        def _():
            fold(sums)
            copy = pltpu.make_async_copy(sums[0], out, sem)
            copy.start()
            copy.wait()

    scalars = pl.BlockSpec(memory_space=pltpu.SMEM)
    sums = pltpu.VMEM((part_rows, width), jnp.float32)
    return pl.pallas_call(
        kernel,
        grid=(span_count,),
        out_shape=jax.ShapeDtypeStruct((part_rows, width), jnp.float32),
        in_specs=[scalars] * (1 + per)
        + [pl.BlockSpec((span_len, width), lambda b: (b, 0)), pl.BlockSpec((neg_count, width), lambda b: (b, 0))],
        out_specs=pl.BlockSpec(memory_space=pl.ANY),
        scratch_shapes=[pltpu.VMEM((span_len, width), jnp.float32), pltpu.VMEM((neg_count, width), jnp.float32)]
        + [pltpu.SemaphoreType.DMA]
        + [sums] * (2 + NEG_SUMS),
        compiler_params=params(),
        cost_estimate=pl.CostEstimate(flops=0, bytes_accessed=40 * count * width, transcendentals=0),
        name="scatter_right",
    )(dst, *draws, gy, gn)


def place_of(bucket):
    core = lax.rem(bucket, CORES)
    chip = lax.div(bucket, CORES)
    return {"core": core, "y": lax.rem(chip, SIDE), "z": lax.div(chip, SIDE), "x": lax.axis_index("dom")}


def size_of(axes):
    return math.prod(SIZES[axis] for axis in axes)


def index_of(place, axes):
    index = 0
    for axis in axes:
        index = index * SIZES[axis] + place[axis]
    return index


def peer_of(place, axes, by):
    index = lax.rem(index_of(place, axes) + by, size_of(axes))
    spot = dict(place)
    for axis in reversed(axes):
        spot[axis] = lax.rem(index, SIZES[axis])
        index = lax.div(index, SIZES[axis])
    return {"bucket": (spot["z"] * SIDE + spot["y"]) * CORES + spot["core"], "dom": spot["x"]}


def sum_everywhere(grads):
    rows, width = grads.shape
    half = rows // len(ORDERS)

    def kernel(grad, out, *scratch):
        levels = len(ORDERS[0])
        parts = [scratch[k * levels : (k + 1) * levels] for k in range(len(ORDERS))]
        arrived = [scratch[(len(ORDERS) + k) * levels : (len(ORDERS) + k + 1) * levels] for k in range(len(ORDERS))]
        send_in, recv_in, send_out, recv_out = scratch[2 * len(ORDERS) * levels :]
        place = place_of(lax.axis_index("bucket"))
        barrier = pltpu.get_barrier_semaphore()
        partners = [(("core",), by) for by in range(1, CORES)]
        partners += [(("z", "x"), by) for by in range(1, SIDE * SIDE)]
        partners += [(("y", "x"), by) for by in range(1, SIDE * SIDE)]
        greeted = len(partners)
        for axes, by in partners:
            pl.semaphore_signal(barrier, inc=1, device_id=peer_of(place, axes, by), device_id_type=MESH)
        pl.semaphore_wait(barrier, greeted)

        def copy(source, target, sends, recvs, k, level, by, axis):
            return pltpu.make_async_remote_copy(
                src_ref=source,
                dst_ref=target,
                send_sem=sends.at[k, level, by],
                recv_sem=recvs.at[k, level, by],
                device_id=peer_of(place, axis, by),
                device_id_type=MESH,
            )

        lows = [k * half for k in range(len(ORDERS))]
        starts = [[] for _ in ORDERS]
        for level in range(levels):
            copies = []
            for k, order in enumerate(ORDERS):
                axis = order[level]
                size = size_of(axis)
                block = half // math.prod(size_of(a) for a in order[: level + 1])
                source = grad if level == 0 else parts[k][level - 1]
                base = lows[k] if level == 0 else 0
                for by in range(1, size):
                    other = lax.rem(index_of(place, axis) + by, size)
                    c = copy(
                        source.at[pl.ds(pl.multiple_of(base + other * block, 8), block), :],
                        arrived[k][level].at[by - 1],
                        send_in, recv_in, k, level, by, axis,
                    )
                    c.start()
                    copies.append(c)
            for c in copies:
                c.wait()
            for k, order in enumerate(ORDERS):
                axis = order[level]
                size = size_of(axis)
                block = half // math.prod(size_of(a) for a in order[: level + 1])
                source = grad if level == 0 else parts[k][level - 1]
                base = lows[k] if level == 0 else 0
                own = source[pl.ds(pl.multiple_of(base + index_of(place, axis) * block, 8), block), :]
                for by in range(1, size):
                    own = own + arrived[k][level][by - 1]
                starts[k].append(index_of(place, axis) * block)
                if level < levels - 1:
                    parts[k][level][...] = own
                else:
                    first = lows[k] + sum(starts[k])
                    out[pl.ds(pl.multiple_of(first, 8), block), :] = own
        for level in reversed(range(levels)):
            copies = []
            for k, order in enumerate(ORDERS):
                axis = order[level]
                block = half // math.prod(size_of(a) for a in order[: level + 1])
                first = lows[k] + sum(starts[k][: level + 1])
                where = out.at[pl.ds(pl.multiple_of(first, 8), block), :]
                for by in range(1, size_of(axis)):
                    c = copy(where, where, send_out, recv_out, k, level, by, axis)
                    c.start()
                    copies.append(c)
            for c in copies:
                c.wait()

    parts, arrived = [], []
    for order in ORDERS:
        for level in range(len(order)):
            block = half // math.prod(size_of(a) for a in order[: level + 1])
            parts.append(pltpu.VMEM((block, width), jnp.float32))
            arrived.append(pltpu.VMEM((size_of(order[level]) - 1, block, width), jnp.float32))
    whole = pl.BlockSpec(memory_space=pltpu.VMEM)
    sems = pltpu.SemaphoreType.DMA((len(ORDERS), len(ORDERS[0]), SIDE * SIDE))
    return pl.pallas_call(
        kernel,
        out_shape=jax.ShapeDtypeStruct(grads.shape, jnp.float32),
        in_specs=[whole],
        out_specs=whole,
        scratch_shapes=parts + arrived + [sems] * 4,
        compiler_params=pltpu.CompilerParams(
            collective_id=0, has_side_effects=True, vmem_limit_bytes=40 * 1024 * 1024
        ),
        cost_estimate=pl.CostEstimate(flops=2 * rows * width, bytes_accessed=40 * rows * width, transcendentals=0),
        name="relation_sums",
    )(grads)


def body(
    left_table,
    right_table,
    left_state,
    right_state,
    sources,
    targets,
    relation_ids,
    negatives,
    rotation,
    relations,
    relation_state,
):
    trainers = lax.axis_size("bucket")
    left_full = lax.all_gather(left_table, "dom", axis=0, tiled=True)
    right_rows = rotate(right_table, jnp.mod(rotation[0], trainers))
    right_full = lax.all_gather(right_rows, "dom", axis=0, tiled=True)
    span_len = sources.shape[0] // negatives.shape[0]
    part_rows, rel_rows = left_full.shape[0], relations.shape[0]
    x, r = look_up(sources, relation_ids, left_full, relations, span_len)
    left_grad, rel_grad, grad_y, grad_n = score_blocks(
        sources, targets, relation_ids, negatives, x, r, right_full, part_rows, rel_rows, span_len
    )
    left_share = lax.psum_scatter(left_grad, "dom", scatter_dimension=0, tiled=True)
    right_grad = scatter_right(targets, negatives, grad_y, grad_n, part_rows, span_len)
    right_grad, left_share = lax.optimization_barrier((right_grad, left_share))
    right_share = lax.psum_scatter(right_grad, "dom", scatter_dimension=0, tiled=True)
    right_share = rotate(right_share, jnp.mod(-rotation[0], trainers))
    new_left, new_left_acc = adagrad(left_table, left_state, left_share)
    new_right, new_right_acc = adagrad(right_table, right_state, right_share)
    rel_total = sum_everywhere(rel_grad)
    new_rel, new_rel_acc = adagrad(relations, relation_state, rel_total)
    return (new_left, new_right, new_left_acc, new_right_acc, new_rel, new_rel_acc)


def solution(mesh):
    both = ("bucket", "dom")
    return jax.shard_map(
        body,
        mesh=mesh,
        in_specs=(
            P(both, None),
            P(both, None),
            P(both),
            P(both),
            P(both),
            P(both),
            P(both),
            P(both, None),
            P(),
            P(),
            P(),
        ),
        out_specs=(P(both, None), P(both, None), P(both), P(both), P(), P()),
        check_vma=False,
    )
```

```python
import math

import jax
import jax.numpy as jnp
from jax import lax
from jax.experimental import pallas as pl
from jax.experimental.pallas import tpu as pltpu
from jax.sharding import PartitionSpec as P

learn_rate = 0.2
margin_gap = 1.0
TILE = 256
UNROLL = 64
SUMS = 2
NEG_SUMS = 4
VMEM_LIMIT = 60 * 1024 * 1024
MESH = pl.DeviceIdType.MESH
CORES, SIDE = 2, 4
SIZES = {"core": CORES, "y": SIDE, "z": SIDE, "x": SIDE}
ORDERS = (("core", "y", "z", "x"), ("core", "z", "y", "x"), ("core", "y", "z", "x"), ("core", "z", "y", "x"))
NT = (((1,), (1,)), ((), ()))
NN = (((1,), (0,)), ((), ()))


def adagrad(param, state, grad):
    new_state = state + jnp.mean(grad * grad, axis=-1)
    return (param - learn_rate * grad / jnp.sqrt(new_state)[:, None], new_state)


def rotate(array, amount):
    size = lax.axis_size("bucket")

    def move(by):
        if by == 0:
            return lambda a: a
        return lambda a: lax.ppermute(a, "bucket", [(i, (i - by) % size) for i in range(size)])

    return lax.switch(amount, [move(by) for by in range(size)], array)


def split(a):
    hi = a.astype(jnp.bfloat16)
    return hi, (a - hi.astype(jnp.float32)).astype(jnp.bfloat16)


def dot(a, b, dims=NN):
    return lax.dot_general(a, b, dims, preferred_element_type=jnp.float32)


def params(**kw):
    return pltpu.CompilerParams(vmem_limit_bytes=VMEM_LIMIT, **kw)


def look_up(src, rid, left, rel, span_len):
    count = src.shape[0]
    width = left.shape[1]

    def kernel(src, rid, left, rel, x, r):
        base = pl.program_id(0) * span_len

        @pl.loop(0, span_len // UNROLL)
        def _(i):
            e0 = pl.multiple_of(i * UNROLL, UNROLL)
            for s in range(UNROLL):
                e = base + e0 + s
                x[pl.ds(e0 + s, 1), :] = left[pl.ds(src[e], 1), :]
                r[pl.ds(e0 + s, 1), :] = rel[pl.ds(rid[e], 1), :]

    scalars = pl.BlockSpec(memory_space=pltpu.SMEM)
    whole = pl.BlockSpec(memory_space=pltpu.VMEM)
    block = pl.BlockSpec((span_len, width), lambda b: (b, 0))
    return pl.pallas_call(
        kernel,
        grid=(count // span_len,),
        out_shape=[jax.ShapeDtypeStruct((count, width), jnp.float32)] * 2,
        in_specs=[scalars] * 2 + [whole] * 2,
        out_specs=[block] * 2,
        compiler_params=params(),
        cost_estimate=pl.CostEstimate(flops=0, bytes_accessed=10 * count * width, transcendentals=0),
        name="look_up",
    )(src, rid, left, rel)


def fold(sums):
    @pl.loop(0, sums[0].shape[0] // 256)
    def _(i):
        rows = pl.ds(pl.multiple_of(i * 256, 256), 256)
        total = sums[0][rows, :]
        for a in sums[1:]:
            total = total + a[rows, :]
        sums[0][rows, :] = total


def score_blocks(src, dst, rid, neg, x, r, right, left_rows, rel_rows, span_len):
    span_count, neg_count = neg.shape
    count, width = x.shape
    tile = min(TILE, span_len)
    per = neg_count // span_len
    draws = [neg[:, k * span_len : (k + 1) * span_len].reshape(-1) for k in range(per)]
    src, rid = jnp.roll(src, span_len), jnp.roll(rid, span_len)

    def kernel(src, dst, rid, *rest):
        draws, (x, r, right_hbm, gl_hbm, grel_hbm, gy, gn, right, y, n, gx, gg, sems), sums = (
            rest[:per],
            rest[per : per + 13],
            rest[per + 13 :],
        )
        b = pl.program_id(0)
        left_sums, rel_sums = sums[:SUMS], sums[SUMS:]

        def move_rows(i, gathers, scatters):
            e0 = pl.multiple_of(i * UNROLL, UNROLL)
            at = (b if gathers else 0) * span_len + e0
            for s in range(UNROLL):
                if scatters:
                    left_sums[s % SUMS][pl.ds(src[at + s], 1), :] += gx[pl.ds(e0 + s, 1), :]
                    rel_sums[s % SUMS][pl.ds(rid[at + s], 1), :] += gg[pl.ds(e0 + s, 1), :]
                if gathers:
                    y[pl.ds(e0 + s, 1), :] = right[pl.ds(dst[at + s], 1), :]
                    for k in range(per):
                        n[pl.ds(k * span_len + e0 + s, 1), :] = right[pl.ds(draws[k][at + s], 1), :]

        def every_row(gathers, scatters):
            @pl.loop(0, span_len // UNROLL)
            def _(i):
                move_rows(i, gathers, scatters)

        @pl.when(b == 0)
        def _():
            copy = pltpu.make_async_copy(right_hbm, right, sems.at[0])
            copy.start()
            for a in left_sums + rel_sums:
                a[...] = jnp.zeros_like(a)
            copy.wait()

            every_row(True, False)

        @pl.when((b > 0) & (b < span_count))
        def _():
            every_row(True, True)

        @pl.when(b == span_count)
        def _():
            every_row(False, True)
            fold(left_sums)
            fold(rel_sums)
            left_copy = pltpu.make_async_copy(left_sums[0], gl_hbm, sems.at[0])
            rel_copy = pltpu.make_async_copy(rel_sums[0], grel_hbm, sems.at[1])
            left_copy.start()
            rel_copy.start()
            left_copy.wait()
            rel_copy.wait()

        @pl.when(b < span_count)
        def _():
            nh, nl = split(n[...])
            ncat = jnp.concatenate([nh, nl], axis=1)
            acc = jnp.zeros((2 * width, neg_count), jnp.float32)
            acc2 = jnp.zeros((width, neg_count), jnp.float32)
            for t in range(span_len // tile):
                rows = pl.ds(t * tile, tile)
                xv, rv, yv = x[rows, :], r[rows, :], y[rows, :]
                q = xv * rv
                pos = jnp.sum(q * yv, axis=1, keepdims=True)
                qh, ql = split(q)
                score = dot(jnp.concatenate([qh, ql], axis=1), jnp.concatenate([nh, nh], axis=1), NT) + dot(qh, nl, NT)
                w = jax.nn.sigmoid(score + (margin_gap - pos))
                total = jnp.sum(w, axis=1, keepdims=True) * (1.0 / neg_count)
                wh, wl = split(w)
                a = dot(wh, ncat)
                gq = (a[:, :width] + a[:, width:] + dot(wl, nh)) * (1.0 / neg_count) - total * yv
                gx[rows, :] = gq * rv
                gg[rows, :] = gq * xv
                gy[rows, :] = -total * q
                qth, qtl = split(q.T)
                acc += dot(jnp.concatenate([qth, qtl], axis=0), wh)
                acc2 += dot(qth, wl)
            gn[...] = ((acc[:width] + acc[width:] + acc2) * (1.0 / neg_count)).T

    scalars = pl.BlockSpec(memory_space=pltpu.SMEM)
    anywhere = pl.BlockSpec(memory_space=pl.ANY)
    last = span_count - 1
    edge = pl.BlockSpec((span_len, width), lambda b: (jnp.minimum(b, last), 0))
    negs = pl.BlockSpec((neg_count, width), lambda b: (jnp.minimum(b, last), 0))
    edge_rows = pltpu.VMEM((span_len, width), jnp.float32)
    neg_rows = pltpu.VMEM((neg_count, width), jnp.float32)
    return pl.pallas_call(
        kernel,
        grid=(span_count + 1,),
        out_shape=[
            jax.ShapeDtypeStruct(shape, jnp.float32)
            for shape in ((left_rows, width), (rel_rows, width), (count, width), (span_count * neg_count, width))
        ],
        in_specs=[scalars] * (3 + per) + [edge] * 2 + [anywhere],
        out_specs=[anywhere] * 2 + [edge, negs],
        scratch_shapes=[
            pltpu.VMEM(right.shape, jnp.float32),
            edge_rows,
            neg_rows,
            edge_rows,
            edge_rows,
            pltpu.SemaphoreType.DMA((2,)),
        ]
        + [pltpu.VMEM((left_rows, width), jnp.float32)] * SUMS
        + [pltpu.VMEM((rel_rows, width), jnp.float32)] * SUMS,
        compiler_params=params(),
        name="score_blocks",
    )(src, dst, rid, *draws, x, r, right)


def scatter_right(dst, neg, gy, gn, part_rows, span_len):
    count, width = gy.shape
    span_count, neg_count = neg.shape
    per = neg_count // span_len
    draws = [neg[:, k * span_len : (k + 1) * span_len].reshape(-1) for k in range(per)]

    def kernel(dst, *rest):
        draws, (gy_block, gn_block, out, gy, gn, sem), sums = rest[:per], rest[per : per + 6], rest[per + 6 :]
        b = pl.program_id(0)
        edge_sums, neg_sums = sums[:2], sums[2:]
        gy[...] = gy_block[...]
        gn[...] = gn_block[...]

        @pl.when(b == 0)
        def _():
            for a in sums:
                a[...] = jnp.zeros_like(a)

        @pl.loop(0, span_len // UNROLL)
        def _(i):
            e0 = pl.multiple_of(i * UNROLL, UNROLL)
            at = b * span_len + e0
            for s in range(UNROLL):
                edge_sums[s % 2][pl.ds(dst[at + s], 1), :] += gy[pl.ds(e0 + s, 1), :]
                for k in range(per):
                    row = draws[k][at + s]
                    neg_sums[(per * s + k) % len(neg_sums)][pl.ds(row, 1), :] += gn[pl.ds(k * span_len + e0 + s, 1), :]

        @pl.when(b == span_count - 1)
        def _():
            fold(sums)
            copy = pltpu.make_async_copy(sums[0], out, sem)
            copy.start()
            copy.wait()

    scalars = pl.BlockSpec(memory_space=pltpu.SMEM)
    sums = pltpu.VMEM((part_rows, width), jnp.float32)
    return pl.pallas_call(
        kernel,
        grid=(span_count,),
        out_shape=jax.ShapeDtypeStruct((part_rows, width), jnp.float32),
        in_specs=[scalars] * (1 + per)
        + [pl.BlockSpec((span_len, width), lambda b: (b, 0)), pl.BlockSpec((neg_count, width), lambda b: (b, 0))],
        out_specs=pl.BlockSpec(memory_space=pl.ANY),
        scratch_shapes=[pltpu.VMEM((span_len, width), jnp.float32), pltpu.VMEM((neg_count, width), jnp.float32)]
        + [pltpu.SemaphoreType.DMA]
        + [sums] * (2 + NEG_SUMS),
        compiler_params=params(),
        cost_estimate=pl.CostEstimate(flops=0, bytes_accessed=40 * count * width, transcendentals=0),
        name="scatter_right",
    )(dst, *draws, gy, gn)


def split_place(bucket):
    core = lax.rem(bucket, CORES)
    chip = lax.div(bucket, CORES)
    return {"core": core, "y": lax.rem(chip, SIDE), "z": lax.div(chip, SIDE), "x": lax.axis_index("dom")}


def peer_of(place, axis, by):
    size = SIZES[axis]
    spot = dict(place)
    spot[axis] = lax.rem(place[axis] + by, size)
    return {"bucket": (spot["z"] * SIDE + spot["y"]) * CORES + spot["core"], "dom": spot["x"]}


def sum_everywhere(grads):
    rows, width = grads.shape
    half = rows // len(ORDERS)

    def kernel(grad, out, *scratch):
        levels = len(ORDERS[0])
        parts = [scratch[k * levels : (k + 1) * levels] for k in range(len(ORDERS))]
        arrived = [scratch[(len(ORDERS) + k) * levels : (len(ORDERS) + k + 1) * levels] for k in range(len(ORDERS))]
        send_in, recv_in, send_out, recv_out = scratch[2 * len(ORDERS) * levels :]
        place = split_place(lax.axis_index("bucket"))
        barrier = pltpu.get_barrier_semaphore()
        greeted = 0
        for axis, size in SIZES.items():
            for by in range(1, size):
                pl.semaphore_signal(barrier, inc=1, device_id=peer_of(place, axis, by), device_id_type=MESH)
                greeted += 1
        pl.semaphore_wait(barrier, greeted)

        def copy(source, target, sends, recvs, k, level, by, axis):
            return pltpu.make_async_remote_copy(
                src_ref=source,
                dst_ref=target,
                send_sem=sends.at[k, level, by],
                recv_sem=recvs.at[k, level, by],
                device_id=peer_of(place, axis, by),
                device_id_type=MESH,
            )

        lows = [k * half for k in range(len(ORDERS))]
        starts = [[] for _ in ORDERS]
        flying = [[] for _ in ORDERS]

        def block_of(k, level):
            return half // math.prod(SIZES[a] for a in ORDERS[k][: level + 1])

        def held(k, level):
            return (grad, lows[k]) if level == 0 else (parts[k][level - 1], 0)

        def spread(k, level):
            axis, block = ORDERS[k][level], block_of(k, level)
            source, base = held(k, level)
            for by in range(1, SIZES[axis]):
                at = base + lax.rem(place[axis] + by, SIZES[axis]) * block
                piece = source.at[pl.ds(pl.multiple_of(at, 8), block), :]
                c = copy(piece, arrived[k][level].at[by - 1], send_in, recv_in, k, level, by, axis)
                c.start()
                flying[k].append(c)

        def add_up(k, level):
            axis, block = ORDERS[k][level], block_of(k, level)
            source, base = held(k, level)
            own = source[pl.ds(pl.multiple_of(base + place[axis] * block, 8), block), :]
            for by in range(1, SIZES[axis]):
                own = own + arrived[k][level][by - 1]
            starts[k].append(place[axis] * block)
            if level < levels - 1:
                parts[k][level][...] = own
            else:
                out[pl.ds(pl.multiple_of(lows[k] + sum(starts[k]), 8), block), :] = own

        def collect(k, level):
            first = lows[k] + sum(starts[k][: level + 1])
            where = out.at[pl.ds(pl.multiple_of(first, 8), block_of(k, level)), :]
            for by in range(1, SIZES[ORDERS[k][level]]):
                c = copy(where, where, send_out, recv_out, k, level, by, ORDERS[k][level])
                c.start()
                flying[k].append(c)

        for stage in range(2 * levels + 1):
            for k in range(len(ORDERS)):
                for c in flying[k]:
                    c.wait()
                flying[k].clear()
                if 0 < stage <= levels:
                    add_up(k, stage - 1)
                if stage < levels:
                    spread(k, stage)
                elif stage < 2 * levels:
                    collect(k, 2 * levels - 1 - stage)

    parts, arrived = [], []
    for order in ORDERS:
        for level in range(len(order)):
            block = half // math.prod(SIZES[a] for a in order[: level + 1])
            parts.append(pltpu.VMEM((block, width), jnp.float32))
            arrived.append(pltpu.VMEM((SIZES[order[level]] - 1, block, width), jnp.float32))
    whole = pl.BlockSpec(memory_space=pltpu.VMEM)
    sems = pltpu.SemaphoreType.DMA((len(ORDERS), len(ORDERS[0]), SIDE))
    return pl.pallas_call(
        kernel,
        out_shape=jax.ShapeDtypeStruct(grads.shape, jnp.float32),
        in_specs=[whole],
        out_specs=whole,
        scratch_shapes=parts + arrived + [sems] * 4,
        compiler_params=pltpu.CompilerParams(
            collective_id=0, has_side_effects=True, vmem_limit_bytes=40 * 1024 * 1024
        ),
        cost_estimate=pl.CostEstimate(flops=2 * rows * width, bytes_accessed=40 * rows * width, transcendentals=0),
        name="relation_sums",
    )(grads)


def body(
    left_table,
    right_table,
    left_state,
    right_state,
    sources,
    targets,
    relation_ids,
    negatives,
    rotation,
    relations,
    relation_state,
):
    trainers = lax.axis_size("bucket")
    left_full = lax.all_gather(left_table, "dom", axis=0, tiled=True)
    right_rows = rotate(right_table, jnp.mod(rotation[0], trainers))
    right_full = lax.all_gather(right_rows, "dom", axis=0, tiled=True)
    span_len = sources.shape[0] // negatives.shape[0]
    part_rows, rel_rows = left_full.shape[0], relations.shape[0]
    x, r = look_up(sources, relation_ids, left_full, relations, span_len)
    left_grad, rel_grad, grad_y, grad_n = score_blocks(
        sources, targets, relation_ids, negatives, x, r, right_full, part_rows, rel_rows, span_len
    )
    left_share = lax.psum_scatter(left_grad, "dom", scatter_dimension=0, tiled=True)
    right_grad = scatter_right(targets, negatives, grad_y, grad_n, part_rows, span_len)
    right_grad, left_share = lax.optimization_barrier((right_grad, left_share))
    right_share = lax.psum_scatter(right_grad, "dom", scatter_dimension=0, tiled=True)
    right_share = rotate(right_share, jnp.mod(-rotation[0], trainers))
    new_left, new_left_acc = adagrad(left_table, left_state, left_share)
    new_right, new_right_acc = adagrad(right_table, right_state, right_share)
    rel_total = sum_everywhere(rel_grad)
    new_rel, new_rel_acc = adagrad(relations, relation_state, rel_total)
    return (new_left, new_right, new_left_acc, new_right_acc, new_rel, new_rel_acc)


def solution(mesh):
    both = ("bucket", "dom")
    return jax.shard_map(
        body,
        mesh=mesh,
        in_specs=(
            P(both, None),
            P(both, None),
            P(both),
            P(both),
            P(both),
            P(both),
            P(both),
            P(both, None),
            P(),
            P(),
            P(),
        ),
        out_specs=(P(both, None), P(both, None), P(both), P(both), P(), P()),
        check_vma=False,
    )
```

```python
import math

import jax
import jax.numpy as jnp
from jax import lax
from jax.experimental import pallas as pl
from jax.experimental.pallas import tpu as pltpu
from jax.sharding import PartitionSpec as P

learn_rate = 0.2
margin_gap = 1.0
TILE = 256
UNROLL = 128
SUMS = 2
NEG_SUMS = 4
VMEM_LIMIT = 60 * 1024 * 1024
MESH = pl.DeviceIdType.MESH
CORES, SIDE = 2, 4
SIZES = {"core": CORES, "y": SIDE, "z": SIDE, "x": SIDE}
ORDERS = (("core", "y", "z", "x"), ("core", "z", "y", "x"), ("core", "y", "z", "x"), ("core", "z", "y", "x"))
NT = (((1,), (1,)), ((), ()))
NN = (((1,), (0,)), ((), ()))


def adagrad(param, state, grad):
    new_state = state + jnp.mean(grad * grad, axis=-1)
    return (param - learn_rate * grad / jnp.sqrt(new_state)[:, None], new_state)


def rotate(array, amount):
    size = lax.axis_size("bucket")

    def move(by):
        if by == 0:
            return lambda a: a
        return lambda a: lax.ppermute(a, "bucket", [(i, (i - by) % size) for i in range(size)])

    return lax.switch(amount, [move(by) for by in range(size)], array)


def split(a):
    hi = a.astype(jnp.bfloat16)
    return hi, (a - hi.astype(jnp.float32)).astype(jnp.bfloat16)


def dot(a, b, dims=NN):
    return lax.dot_general(a, b, dims, preferred_element_type=jnp.float32)


def params(**kw):
    return pltpu.CompilerParams(vmem_limit_bytes=VMEM_LIMIT, **kw)


def look_up(src, rid, left, rel, span_len):
    count = src.shape[0]
    width = left.shape[1]

    def kernel(src, rid, left, rel, x, r):
        base = pl.program_id(0) * span_len

        @pl.loop(0, span_len // UNROLL)
        def _(i):
            e0 = pl.multiple_of(i * UNROLL, UNROLL)
            for s in range(UNROLL):
                e = base + e0 + s
                x[pl.ds(e0 + s, 1), :] = left[pl.ds(src[e], 1), :]
                r[pl.ds(e0 + s, 1), :] = rel[pl.ds(rid[e], 1), :]

    scalars = pl.BlockSpec(memory_space=pltpu.SMEM)
    whole = pl.BlockSpec(memory_space=pltpu.VMEM)
    block = pl.BlockSpec((span_len, width), lambda b: (b, 0))
    return pl.pallas_call(
        kernel,
        grid=(count // span_len,),
        out_shape=[jax.ShapeDtypeStruct((count, width), jnp.float32)] * 2,
        in_specs=[scalars] * 2 + [whole] * 2,
        out_specs=[block] * 2,
        compiler_params=params(),
        cost_estimate=pl.CostEstimate(flops=0, bytes_accessed=10 * count * width, transcendentals=0),
        name="look_up",
    )(src, rid, left, rel)


def fold(sums):
    @pl.loop(0, sums[0].shape[0] // 256)
    def _(i):
        rows = pl.ds(pl.multiple_of(i * 256, 256), 256)
        total = sums[0][rows, :]
        for a in sums[1:]:
            total = total + a[rows, :]
        sums[0][rows, :] = total


def score_blocks(src, dst, rid, neg, x, r, right, left_rows, rel_rows, span_len):
    span_count, neg_count = neg.shape
    count, width = x.shape
    tile = min(TILE, span_len)
    per = neg_count // span_len
    draws = [neg[:, k * span_len : (k + 1) * span_len].reshape(-1) for k in range(per)]
    src, rid = jnp.roll(src, span_len), jnp.roll(rid, span_len)

    def kernel(src, dst, rid, *rest):
        draws, (x, r, right_hbm, gl_hbm, grel_hbm, gy, gn, right, y, n, gx, gg, sems), sums = (
            rest[:per],
            rest[per : per + 13],
            rest[per + 13 :],
        )
        b = pl.program_id(0)
        left_sums, rel_sums = sums[:SUMS], sums[SUMS:]

        def move_rows(i, gathers, scatters):
            e0 = pl.multiple_of(i * UNROLL, UNROLL)
            at = (b if gathers else 0) * span_len + e0
            for s in range(UNROLL):
                if scatters:
                    left_sums[s % SUMS][pl.ds(src[at + s], 1), :] += gx[pl.ds(e0 + s, 1), :]
                    rel_sums[s % SUMS][pl.ds(rid[at + s], 1), :] += gg[pl.ds(e0 + s, 1), :]
                if gathers:
                    y[pl.ds(e0 + s, 1), :] = right[pl.ds(dst[at + s], 1), :]
                    for k in range(per):
                        n[pl.ds(k * span_len + e0 + s, 1), :] = right[pl.ds(draws[k][at + s], 1), :]

        def every_row(gathers, scatters):
            @pl.loop(0, span_len // UNROLL)
            def _(i):
                move_rows(i, gathers, scatters)

        @pl.when(b == 0)
        def _():
            copy = pltpu.make_async_copy(right_hbm, right, sems.at[0])
            copy.start()
            for a in left_sums + rel_sums:
                a[...] = jnp.zeros_like(a)
            copy.wait()

            every_row(True, False)

        @pl.when((b > 0) & (b < span_count))
        def _():
            every_row(True, True)

        @pl.when(b == span_count)
        def _():
            every_row(False, True)
            fold(left_sums)
            fold(rel_sums)
            left_copy = pltpu.make_async_copy(left_sums[0], gl_hbm, sems.at[0])
            rel_copy = pltpu.make_async_copy(rel_sums[0], grel_hbm, sems.at[1])
            left_copy.start()
            rel_copy.start()
            left_copy.wait()
            rel_copy.wait()

        @pl.when(b < span_count)
        def _():
            nh, nl = split(n[...])
            ncat = jnp.concatenate([nh, nl], axis=1)
            acc = jnp.zeros((2 * width, neg_count), jnp.float32)
            acc2 = jnp.zeros((width, neg_count), jnp.float32)
            for t in range(span_len // tile):
                rows = pl.ds(t * tile, tile)
                xv, rv, yv = x[rows, :], r[rows, :], y[rows, :]
                q = xv * rv
                pos = jnp.sum(q * yv, axis=1, keepdims=True)
                qh, ql = split(q)
                score = dot(jnp.concatenate([qh, ql], axis=1), jnp.concatenate([nh, nh], axis=1), NT) + dot(qh, nl, NT)
                w = jax.nn.sigmoid(score + (margin_gap - pos))
                total = jnp.sum(w, axis=1, keepdims=True) * (1.0 / neg_count)
                wh, wl = split(w)
                a = dot(wh, ncat)
                gq = (a[:, :width] + a[:, width:] + dot(wl, nh)) * (1.0 / neg_count) - total * yv
                gx[rows, :] = gq * rv
                gg[rows, :] = gq * xv
                gy[rows, :] = -total * q
                qth, qtl = split(q.T)
                acc += dot(jnp.concatenate([qth, qtl], axis=0), wh)
                acc2 += dot(qth, wl)
            gn[...] = ((acc[:width] + acc[width:] + acc2) * (1.0 / neg_count)).T

    scalars = pl.BlockSpec(memory_space=pltpu.SMEM)
    anywhere = pl.BlockSpec(memory_space=pl.ANY)
    last = span_count - 1
    edge = pl.BlockSpec((span_len, width), lambda b: (jnp.minimum(b, last), 0))
    negs = pl.BlockSpec((neg_count, width), lambda b: (jnp.minimum(b, last), 0))
    edge_rows = pltpu.VMEM((span_len, width), jnp.float32)
    neg_rows = pltpu.VMEM((neg_count, width), jnp.float32)
    return pl.pallas_call(
        kernel,
        grid=(span_count + 1,),
        out_shape=[
            jax.ShapeDtypeStruct(shape, jnp.float32)
            for shape in ((left_rows, width), (rel_rows, width), (count, width), (span_count * neg_count, width))
        ],
        in_specs=[scalars] * (3 + per) + [edge] * 2 + [anywhere],
        out_specs=[anywhere] * 2 + [edge, negs],
        scratch_shapes=[
            pltpu.VMEM(right.shape, jnp.float32),
            edge_rows,
            neg_rows,
            edge_rows,
            edge_rows,
            pltpu.SemaphoreType.DMA((2,)),
        ]
        + [pltpu.VMEM((left_rows, width), jnp.float32)] * SUMS
        + [pltpu.VMEM((rel_rows, width), jnp.float32)] * SUMS,
        compiler_params=params(),
        name="score_blocks",
    )(src, dst, rid, *draws, x, r, right)


def scatter_right(dst, neg, gy, gn, part_rows, span_len):
    count, width = gy.shape
    span_count, neg_count = neg.shape
    per = neg_count // span_len
    draws = [neg[:, k * span_len : (k + 1) * span_len].reshape(-1) for k in range(per)]

    def kernel(dst, *rest):
        draws, (gy_block, gn_block, out, gy, gn, sem), sums = rest[:per], rest[per : per + 6], rest[per + 6 :]
        b = pl.program_id(0)
        edge_sums, neg_sums = sums[:2], sums[2:]
        gy[...] = gy_block[...]
        gn[...] = gn_block[...]

        @pl.when(b == 0)
        def _():
            for a in sums:
                a[...] = jnp.zeros_like(a)

        @pl.loop(0, span_len // UNROLL)
        def _(i):
            e0 = pl.multiple_of(i * UNROLL, UNROLL)
            at = b * span_len + e0
            for s in range(UNROLL):
                edge_sums[s % 2][pl.ds(dst[at + s], 1), :] += gy[pl.ds(e0 + s, 1), :]
                for k in range(per):
                    row = draws[k][at + s]
                    neg_sums[(per * s + k) % len(neg_sums)][pl.ds(row, 1), :] += gn[pl.ds(k * span_len + e0 + s, 1), :]

        @pl.when(b == span_count - 1)
        def _():
            fold(sums)
            copy = pltpu.make_async_copy(sums[0], out, sem)
            copy.start()
            copy.wait()

    scalars = pl.BlockSpec(memory_space=pltpu.SMEM)
    sums = pltpu.VMEM((part_rows, width), jnp.float32)
    return pl.pallas_call(
        kernel,
        grid=(span_count,),
        out_shape=jax.ShapeDtypeStruct((part_rows, width), jnp.float32),
        in_specs=[scalars] * (1 + per)
        + [pl.BlockSpec((span_len, width), lambda b: (b, 0)), pl.BlockSpec((neg_count, width), lambda b: (b, 0))],
        out_specs=pl.BlockSpec(memory_space=pl.ANY),
        scratch_shapes=[pltpu.VMEM((span_len, width), jnp.float32), pltpu.VMEM((neg_count, width), jnp.float32)]
        + [pltpu.SemaphoreType.DMA]
        + [sums] * (2 + NEG_SUMS),
        compiler_params=params(),
        cost_estimate=pl.CostEstimate(flops=0, bytes_accessed=40 * count * width, transcendentals=0),
        name="scatter_right",
    )(dst, *draws, gy, gn)


def split_place(bucket):
    core = lax.rem(bucket, CORES)
    chip = lax.div(bucket, CORES)
    return {"core": core, "y": lax.rem(chip, SIDE), "z": lax.div(chip, SIDE), "x": lax.axis_index("dom")}


def peer_of(place, axis, by):
    size = SIZES[axis]
    spot = dict(place)
    spot[axis] = lax.rem(place[axis] + by, size)
    return {"bucket": (spot["z"] * SIDE + spot["y"]) * CORES + spot["core"], "dom": spot["x"]}


def sum_everywhere(grads):
    rows, width = grads.shape
    half = rows // len(ORDERS)

    def kernel(grad, out, *scratch):
        levels = len(ORDERS[0])
        parts = [scratch[k * levels : (k + 1) * levels] for k in range(len(ORDERS))]
        arrived = [scratch[(len(ORDERS) + k) * levels : (len(ORDERS) + k + 1) * levels] for k in range(len(ORDERS))]
        send_in, recv_in, send_out, recv_out = scratch[2 * len(ORDERS) * levels :]
        place = split_place(lax.axis_index("bucket"))
        barrier = pltpu.get_barrier_semaphore()
        greeted = 0
        for axis, size in SIZES.items():
            for by in range(1, size):
                pl.semaphore_signal(barrier, inc=1, device_id=peer_of(place, axis, by), device_id_type=MESH)
                greeted += 1
        pl.semaphore_wait(barrier, greeted)

        def copy(source, target, sends, recvs, k, level, by, axis):
            return pltpu.make_async_remote_copy(
                src_ref=source,
                dst_ref=target,
                send_sem=sends.at[k, level, by],
                recv_sem=recvs.at[k, level, by],
                device_id=peer_of(place, axis, by),
                device_id_type=MESH,
            )

        lows = [k * half for k in range(len(ORDERS))]
        starts = [[] for _ in ORDERS]
        flying = [[] for _ in ORDERS]

        def block_of(k, level):
            return half // math.prod(SIZES[a] for a in ORDERS[k][: level + 1])

        def held(k, level):
            return (grad, lows[k]) if level == 0 else (parts[k][level - 1], 0)

        def spread(k, level):
            axis, block = ORDERS[k][level], block_of(k, level)
            source, base = held(k, level)
            for by in range(1, SIZES[axis]):
                at = base + lax.rem(place[axis] + by, SIZES[axis]) * block
                piece = source.at[pl.ds(pl.multiple_of(at, 8), block), :]
                c = copy(piece, arrived[k][level].at[by - 1], send_in, recv_in, k, level, by, axis)
                c.start()
                flying[k].append(c)

        def add_up(k, level):
            axis, block = ORDERS[k][level], block_of(k, level)
            source, base = held(k, level)
            own = source[pl.ds(pl.multiple_of(base + place[axis] * block, 8), block), :]
            for by in range(1, SIZES[axis]):
                own = own + arrived[k][level][by - 1]
            starts[k].append(place[axis] * block)
            if level < levels - 1:
                parts[k][level][...] = own
            else:
                out[pl.ds(pl.multiple_of(lows[k] + sum(starts[k]), 8), block), :] = own

        def collect(k, level):
            first = lows[k] + sum(starts[k][: level + 1])
            where = out.at[pl.ds(pl.multiple_of(first, 8), block_of(k, level)), :]
            for by in range(1, SIZES[ORDERS[k][level]]):
                c = copy(where, where, send_out, recv_out, k, level, by, ORDERS[k][level])
                c.start()
                flying[k].append(c)

        for stage in range(2 * levels + 1):
            for k in range(len(ORDERS)):
                for c in flying[k]:
                    c.wait()
                flying[k].clear()
                if 0 < stage <= levels:
                    add_up(k, stage - 1)
                if stage < levels:
                    spread(k, stage)
                elif stage < 2 * levels:
                    collect(k, 2 * levels - 1 - stage)

    parts, arrived = [], []
    for order in ORDERS:
        for level in range(len(order)):
            block = half // math.prod(SIZES[a] for a in order[: level + 1])
            parts.append(pltpu.VMEM((block, width), jnp.float32))
            arrived.append(pltpu.VMEM((SIZES[order[level]] - 1, block, width), jnp.float32))
    whole = pl.BlockSpec(memory_space=pltpu.VMEM)
    sems = pltpu.SemaphoreType.DMA((len(ORDERS), len(ORDERS[0]), SIDE))
    return pl.pallas_call(
        kernel,
        out_shape=jax.ShapeDtypeStruct(grads.shape, jnp.float32),
        in_specs=[whole],
        out_specs=whole,
        scratch_shapes=parts + arrived + [sems] * 4,
        compiler_params=pltpu.CompilerParams(
            collective_id=0, has_side_effects=True, vmem_limit_bytes=40 * 1024 * 1024
        ),
        cost_estimate=pl.CostEstimate(flops=2 * rows * width, bytes_accessed=40 * rows * width, transcendentals=0),
        name="relation_sums",
    )(grads)


def body(
    left_table,
    right_table,
    left_state,
    right_state,
    sources,
    targets,
    relation_ids,
    negatives,
    rotation,
    relations,
    relation_state,
):
    trainers = lax.axis_size("bucket")
    left_full = lax.all_gather(left_table, "dom", axis=0, tiled=True)
    right_rows = rotate(right_table, jnp.mod(rotation[0], trainers))
    right_full = lax.all_gather(right_rows, "dom", axis=0, tiled=True)
    span_len = sources.shape[0] // negatives.shape[0]
    part_rows, rel_rows = left_full.shape[0], relations.shape[0]
    x, r = look_up(sources, relation_ids, left_full, relations, span_len)
    left_grad, rel_grad, grad_y, grad_n = score_blocks(
        sources, targets, relation_ids, negatives, x, r, right_full, part_rows, rel_rows, span_len
    )
    left_share = lax.psum_scatter(left_grad, "dom", scatter_dimension=0, tiled=True)
    right_grad = scatter_right(targets, negatives, grad_y, grad_n, part_rows, span_len)
    right_grad, left_share = lax.optimization_barrier((right_grad, left_share))
    right_share = lax.psum_scatter(right_grad, "dom", scatter_dimension=0, tiled=True)
    right_share = rotate(right_share, jnp.mod(-rotation[0], trainers))
    new_left, new_left_acc = adagrad(left_table, left_state, left_share)
    new_right, new_right_acc = adagrad(right_table, right_state, right_share)
    rel_total = sum_everywhere(rel_grad)
    new_rel, new_rel_acc = adagrad(relations, relation_state, rel_total)
    return (new_left, new_right, new_left_acc, new_right_acc, new_rel, new_rel_acc)


def solution(mesh):
    both = ("bucket", "dom")
    return jax.shard_map(
        body,
        mesh=mesh,
        in_specs=(
            P(both, None),
            P(both, None),
            P(both),
            P(both),
            P(both),
            P(both),
            P(both),
            P(both, None),
            P(),
            P(),
            P(),
        ),
        out_specs=(P(both, None), P(both, None), P(both), P(both), P(), P()),
        check_vma=False,
    )
```
